256 devices in a mesh: fluid: 64 (over z, x, core), sect: 4 (over y).
Axes of the slice: x: 4, y: 4, z: 8, core: 2. Of those that a mesh axis runs over, the one named last changes fastest.
Arguments:
- density: float32 [256, 256, 128], P('fluid', 'sect'), may hold values from 0.6 to 1.8
- velocity: float32 [3, 256, 256, 128], P(None, 'fluid', 'sect'), may hold values from -3 to 3
- pressure: float32 [256, 256, 128], P('fluid', 'sect'), may hold values from 0.6 to 3
- deck_disp: float32 [4096, 512], P('fluid', 'sect'), may hold values from -4 to 4
- deck_prev: float32 [4096, 512], P('fluid', 'sect'), may hold values from -4 to 4
- stay_stiff: float32 [168], replicated, may hold values from 0.5 to 4
- stay_tension: float32 [168], replicated, may hold values from 1 to 4
- anchor_node: int32 [168], replicated, may hold values from 0 to 2097151, as said below
- failed_stay: int32 [1], replicated, may hold values from 0 to 167
- facet_cells: int32 [32768, 128], P(('fluid', 'sect')), may hold values from 0 to 255
- facet_owner: int32 [32768, 1], P(('fluid', 'sect')), may hold values from 0 to 63; in each aligned block of 128 rows (0 to 127, 128 to 255, ...) at most 2 rows name the same one
- facet_row: int32 [32768], P(('fluid', 'sect')), may hold values from 0 to 63
- facet_count: int32 [256], P(('fluid', 'sect')), may hold values from 1 to 128, 13107 in all
Outputs:
- fields: float32 [5, 256, 256, 128], P(None, 'fluid', 'sect')
- deck_next: float32 [4096, 512], P('fluid', 'sect')
- facet_disp: float32 [32768, 128], P(('fluid', 'sect'))
The draws below stay inside these ranges and needn't reach their ends.
Inputs may be any that keep to these rules, and one draw needn't show every extreme that they name: `facet_owner`: among the 128 slots of one device every owner index appears exactly 2 times. `facet_count`: the slots below a device's count are live; the counts of all devices sum to 13107. `anchor_node`: distinct deck nodes, numbered row by row over the 4096 x 512 deck.
All inputs are finite; a program needn't handle non-finite values.
Results may differ from the reference program's by a relative error of at most 0.000071.
Values sent between devices are 32-bit elements; how exact they have to be, the bound alone decides.
No kernel may reach another device: no remote copies, remote signals or barrier semaphores. Data moves between devices by JAX's collectives and lax.ppermute only.
A program may use at most 64 MiB of HBM per device.

```python
import math
import jax
import jax.numpy as jnp
import numpy as np
from jax import lax

CX = 4
CY = 64
CZ = 128
SX = 64
SY = 128
STAYS = 168
CAP = 2
SSTEPS = 2
FMAX = 128
LIVE = 13107
NX = 256
NY = 256
NSX = 4096
NSY = 512
N_FLUID = 64
N_SECT = 4
DEVICES = 256


def draw_anchor_node(key, part):
    shuffled = jax.random.permutation(key, SX * N_FLUID * SY * N_SECT)
    return shuffled[:STAYS].astype(jnp.int32)


def touch_ends(result, rng, low, largest):
    shape = result.shape
    spot = [jax.random.randint(jax.random.fold_in(rng, axis), (), 0, shape[axis]) for axis in range(len(shape))]
    result = result.at[tuple(spot)].set(low)
    longest = shape.index(max(shape))
    spot[longest] = (spot[longest] + 1) % shape[longest]
    return result.at[tuple(spot)].set(largest)


def steps_of(rng, extent, pieces, smallest, largest):
    def one(position, blocks):
        draws = jax.random.uniform(jax.random.fold_in(jax.random.fold_in(rng, 6), position), (blocks,), jnp.float32, smallest / len(pieces), largest / len(pieces))
        return jnp.repeat(jnp.exp(draws), extent[position] // blocks).reshape((-1,) + (1,) * (len(extent) - position - 1))

    loudness = one(*pieces[0])
    for cut in pieces[1:]:
        loudness = loudness * one(*cut)
    return loudness


def profile(number_of, total, bound, slope):
    weights = [(1 << 20) // math.isqrt(grade ** slope) + 1 for grade in range(2, number_of + 1)]
    spare, holding = total - bound - (number_of - 1), [1] * (number_of - 1)
    while spare > 0:
        candidates = [i for i in range(number_of - 1) if holding[i] < bound]
        whole, remaining = sum([weights[i] for i in candidates]), spare
        for i in candidates:
            addition = min(bound - holding[i], max(1, remaining * weights[i] // whole), spare)
            holding[i] = holding[i] + addition
            spare = spare - addition
    return np.array([bound] + holding)


def ragged_sizes(stream_key, number_of, total, limit, lean):
    if number_of == 2:
        one = jax.random.randint(stream_key, (), max(1, total - limit), min(limit, total - 1) + 1)
        return jnp.stack([one, total - one])
    tallies = jnp.asarray(profile(number_of, total, limit, lean), jnp.int32)
    twos = (number_of - 1) // 2
    donor, taker = tallies[1:1 + 2 * twos:2], tallies[2:2 + 2 * twos:2]
    margin = jnp.minimum(donor - 1, limit - taker)
    moved = jax.random.randint(jax.random.fold_in(stream_key, 1), (twos,), 0, 1 << 20) % (margin + 1)
    tallies = tallies.at[1:1 + 2 * twos:2].set(donor - moved).at[2:2 + 2 * twos:2].set(taker + moved)
    return tallies[jax.random.permutation(jax.random.fold_in(stream_key, 2), number_of)]


def assign_block(own_key, own, number, rows, number_of, top, bound, skew):
    ranking = jax.random.permutation(own_key, number_of)
    heavy_load, common = portions_of(number_of, rows * top, bound, skew, True), portions_of(number_of, rows * top, bound, skew, False)
    places = jnp.arange(number_of)

    def named(lengths, turn):
        used = int((lengths > 0).sum())
        fixed = max(1, used // 4)
        passed = fixed + (places - fixed + turn * (used - fixed)) % max(1, number_of - fixed)
        return jnp.zeros((number_of,), jnp.int32).at[ranking[jnp.where(places < fixed, places, passed)]].set(jnp.asarray(lengths, jnp.int32))

    lengths = jnp.where(number % 4 == 0, named(heavy_load, number // 4), named(common, number - number // 4 - 1))
    mixed = jax.random.permutation(jax.random.fold_in(own, 3), number_of)
    donor, receiver = mixed[0:number_of // 2 * 2:2], mixed[1:number_of // 2 * 2:2]
    room = jnp.minimum(lengths[donor] - 1, bound - lengths[receiver]) // 2
    room = jnp.where((donor == ranking[0]) | (receiver == ranking[0]) | (lengths[receiver] == 0), 0, jnp.maximum(room, 0))
    passed = jax.random.randint(jax.random.fold_in(own, 4), (number_of // 2,), 0, 1 << 20) % (room + 1)
    lengths = lengths.at[donor].add(-passed).at[receiver].add(passed)
    labels = jnp.searchsorted(jnp.cumsum(lengths), jnp.arange(rows * top), side="right").astype(jnp.int32)
    listing = labels.reshape(top, rows).T
    listing = listing[jax.random.permutation(jax.random.fold_in(own, 1), rows)]
    turn = jax.random.randint(jax.random.fold_in(own, 2), (rows, 1), 0, top)
    return jnp.take_along_axis(listing, (jnp.arange(top)[None, :] + turn) % top, axis=1)


def portions_of(amount, total, most, lean, full):
    loads = [(1 << 20) // math.isqrt(rank ** lean) + 1 for rank in range(1, amount + 1)]
    largest = most if full else min(most, max(-(-total // amount), total * loads[0] // sum(loads)))
    least = 1 if total - largest >= amount - 1 else 0
    given, rest = [largest] + [least] * (amount - 1), total - largest - least * (amount - 1)
    while rest > 0:
        free = [i for i in range(1, amount) if given[i] < largest] or [i for i in range(1, amount) if given[i] < most]
        mass, budget = sum([loads[i] for i in free]), rest
        for i in free:
            more = min(most - given[i], max(1, budget * loads[i] // mass), rest)
            given[i] = given[i] + more
            rest = rest - more
    return np.array(given)


def noise(rng, extent, deviation, limit, cuts=(), kind=jnp.bfloat16):
    level = steps_of(rng, extent, cuts, -0.22, 0.18) if cuts else 1.0
    values = jax.random.normal(rng, extent, jnp.float32) * deviation * level
    return jnp.minimum(jnp.maximum(values, -limit), limit).astype(kind)


def setup_inputs(seed: int = 0) -> dict:
    key_of = jax.random.split(jax.random.key(seed), 14)
    density = jnp.clip(jnp.exp(math.log(1.8) - 1.0986122 * jax.random.uniform(key_of[0], (NX, NY, CZ), jnp.float32) ** steps_of(key_of[0], (NX, NY, CZ), ((0, 64), (1, 4)), -0.2, 0.2)), 0.6, 1.8)
    velocity = noise(key_of[1], (3, NX, NY, CZ), 0.25, 3.0, ((1, 64), (2, 4)), jnp.float32)
    pressure = jnp.clip(jnp.exp(math.log(3.0) - 1.60943787 * jax.random.uniform(key_of[2], (NX, NY, CZ), jnp.float32) ** steps_of(key_of[2], (NX, NY, CZ), ((0, 64), (1, 4)), -0.2, 0.2)), 0.6, 3.0)
    deck_disp = noise(key_of[3], (NSX, NSY), 1.0, 4.0, ((0, 64), (1, 4)), jnp.float32)
    deck_prev = noise(key_of[4], (NSX, NSY), 1.0, 4.0, ((0, 64), (1, 4)), jnp.float32)
    stay_stiff = jnp.clip(jnp.exp(jax.random.uniform(key_of[5], (STAYS,), jnp.float32, math.log(0.5), math.log(4.0))), 0.5, 4.0)
    stay_tension = jnp.clip(jnp.exp(jax.random.uniform(key_of[6], (STAYS,), jnp.float32, math.log(1.0), math.log(4.0))), 1.0, 4.0)
    anchor_node = draw_anchor_node(jax.random.fold_in(key_of[13], 71), 0)
    failed_stay = jax.random.randint(key_of[8], (1,), 0, STAYS).astype(jnp.int32)
    facet_cells = touch_ends(jax.random.randint(key_of[9], (DEVICES * FMAX, SY), 0, CX * CY), jax.random.fold_in(key_of[9], 1), 0, (CX * CY) - 1).astype(jnp.int32)
    facet_owner_keys = jax.random.split(jax.random.fold_in(key_of[10], 1), (DEVICES * FMAX) // FMAX)
    facet_owner_turns = jax.random.permutation(jax.random.fold_in(key_of[10], 3), (DEVICES * FMAX) // FMAX)
    facet_owner = jax.vmap(lambda own, number: assign_block(jax.random.fold_in(key_of[10], 2), own, number, FMAX, N_FLUID, 1, CAP, 0))(facet_owner_keys, facet_owner_turns).reshape((DEVICES * FMAX, 1))
    facet_row = touch_ends(jax.random.randint(key_of[11], (DEVICES * FMAX,), 0, SX), jax.random.fold_in(key_of[11], 1), 0, SX - 1).astype(jnp.int32)
    facet_count = ragged_sizes(key_of[12], DEVICES, LIVE, FMAX, 2).astype(jnp.int32)
    return {"density": density, "velocity": velocity, "pressure": pressure, "deck_disp": deck_disp, "deck_prev": deck_prev, "stay_stiff": stay_stiff, "stay_tension": stay_tension, "anchor_node": anchor_node, "failed_stay": failed_stay, "facet_cells": facet_cells, "facet_owner": facet_owner, "facet_row": facet_row, "facet_count": facet_count}


STEP_FLUID = 0.045
STEP_DECK = 0.06
GAMMA_LESS = 0.4
AMBIENT = 1.0

def wall_pad(fields):
    mirror = jnp.array([1.0, 1.0, 1.0, -1.0, 1.0], dtype=fields.dtype).reshape(5, 1, 1, 1)
    return jnp.concatenate([fields[..., :1] * mirror, fields, fields[..., -1:] * mirror], axis=3)

def directional(fields, component):
    density = fields[0]
    normal_speed = fields[component] / density
    kinetic = 0.5 * (fields[1] * fields[1] + fields[2] * fields[2] + fields[3] * fields[3]) / density
    pressure = GAMMA_LESS * (fields[4] - kinetic)
    sound = jnp.sqrt(1.4 * pressure / density)
    fluxes = [fields[component], fields[1] * normal_speed, fields[2] * normal_speed, fields[3] * normal_speed, (fields[4] + pressure) * normal_speed]
    fluxes[component] = fluxes[component] + pressure
    return (jnp.stack(fluxes), jnp.abs(normal_speed) + sound)

def face_flux(left_side, right_side, component):
    flux_left, speed_left = directional(left_side, component)
    flux_right, speed_right = directional(right_side, component)
    return 0.5 * (flux_left + flux_right) - 0.5 * jnp.maximum(speed_left, speed_right) * (right_side - left_side)

def advance(padded):
    extended = wall_pad(padded)
    faces_first = face_flux(extended[:, :-1, 1:-1, 1:-1], extended[:, 1:, 1:-1, 1:-1], 1)
    faces_second = face_flux(extended[:, 1:-1, :-1, 1:-1], extended[:, 1:-1, 1:, 1:-1], 2)
    faces_third = face_flux(extended[:, 1:-1, 1:-1, :-1], extended[:, 1:-1, 1:-1, 1:], 3)
    centre = extended[:, 1:-1, 1:-1, 1:-1]
    change = faces_first[:, 1:] - faces_first[:, :-1] + (faces_second[:, :, 1:] - faces_second[:, :, :-1]) + (faces_third[:, :, :, 1:] - faces_third[:, :, :, :-1])
    return centre - STEP_FLUID * change

def conserved(density, velocity, pressure):
    momentum = density[None] * velocity
    energy = pressure / GAMMA_LESS + 0.5 * density * lax.optimization_barrier(jnp.sum(velocity * velocity, axis=0))
    return jnp.concatenate([density[None], momentum, energy[None]], axis=0)

def pressure_of(fields):
    kinetic = 0.5 * (fields[1] * fields[1] + fields[2] * fields[2] + fields[3] * fields[3]) / fields[0]
    return GAMMA_LESS * (fields[4] - kinetic)

def laplace(field):
    return field[2:, 1:-1] + field[:-2, 1:-1] + field[1:-1, 2:] + field[1:-1, :-2] - 4.0 * field[1:-1, 1:-1]

def reference(density, velocity, pressure, deck_disp, deck_prev, stay_stiff, stay_tension, anchor_node, failed_stay, facet_cells, facet_owner, facet_row, facet_count):
    fields = conserved(density, velocity, pressure)
    starts = jnp.arange(N_FLUID, dtype=jnp.int32) * CX
    for substep in range(2):
        padded = jnp.pad(fields, ((0, 0), (1, 1), (1, 1), (0, 0)), mode='wrap')

        def one_slab(start, padded=padded):
            return advance(lax.dynamic_slice_in_dim(padded, start, CX + 2, axis=1))
        slabs = lax.map(one_slab, starts)
        fields = jnp.moveaxis(slabs, 0, 1).reshape(5, NX, NY, CZ)
    wall_press = pressure_of(fields[:, :, :, 0])
    slot_total = N_FLUID * N_SECT * FMAX
    row_ids = jnp.arange(slot_total, dtype=jnp.int32)
    device = row_ids // FMAX
    slot_index = row_ids % FMAX
    fluid_index = device // N_SECT
    sect_index = device % N_SECT
    local_x = facet_cells // CY
    local_y = facet_cells % CY
    glob_x = fluid_index[:, None] * CX + local_x
    glob_y = sect_index[:, None] * CY + local_y
    samples = wall_press[glob_x, glob_y]
    alive_slot = slot_index < facet_count[device]
    values = jnp.where(alive_slot[:, None], samples - AMBIENT, jnp.zeros_like(samples))
    deck_rowid = facet_owner[:, 0] * SX + facet_row
    segment = deck_rowid * N_SECT + sect_index
    deck_load = jax.ops.segment_sum(values, segment, num_segments=NSX * N_SECT).reshape(NSX, NSY)
    alive_stay = (jnp.arange(STAYS, dtype=jnp.int32) != failed_stay[0]).astype(jnp.float32)
    current = deck_disp
    previous = deck_prev
    for substep in range(SSTEPS):
        bending = laplace(laplace(jnp.pad(current, 2)))
        anchored = current.reshape(-1)[anchor_node]
        stay_force = alive_stay * (stay_tension - stay_stiff * anchored)
        force_field = jnp.zeros((NSX * NSY,), jnp.float32).at[anchor_node].add(stay_force).reshape(NSX, NSY)
        following = 2.0 * current - previous + STEP_DECK * (deck_load + force_field - bending)
        previous = current
        current = following
    deck_view = current.reshape(NSX, N_SECT, SY)
    returned = deck_view[deck_rowid, sect_index]
    facet_disp = jnp.where(alive_slot[:, None], returned, jnp.zeros_like(returned))
    return (fields, current, facet_disp)
```

```python
import jax
import jax.numpy as jnp
from jax import lax
from jax.experimental import pallas as pl
from jax.experimental.pallas import tpu as pltpu
from jax.sharding import PartitionSpec as P

SSTEPS = 2


STEP_FLUID = 0.045
STEP_DECK = 0.06
GAMMA_LESS = 0.4
AMBIENT = 1.0
SLOT_GROUP = 16


def with_halo(cells, sides, width, closed):
    for axis, dim in sides:
        count = lax.axis_size(axis)
        ends = count if closed else count - 1
        head = lax.slice_in_dim(cells, 0, width, axis=dim)
        tail = lax.slice_in_dim(cells, cells.shape[dim] - width, cells.shape[dim], axis=dim)
        cells = jnp.concatenate(
            [
                lax.ppermute(tail, axis, [(i, (i + 1) % count) for i in range(ends)]),
                cells,
                lax.ppermute(head, axis, [((i + 1) % count, i) for i in range(ends)]),
            ],
            axis=dim,
        )
    return cells


YOFF = 8
YROWS = 80
KFL = 0.5 * STEP_FLUID


def euler_prims(rho, m1, m2, m3, en):
    inv = 1.0 / rho
    v1, v2, v3 = m1 * inv, m2 * inv, m3 * inv
    p = GAMMA_LESS * (en - 0.5 * (m1 * v1 + m2 * v2 + m3 * v3))
    return v1, v2, v3, p, jnp.sqrt(1.4 * p * inv)


def from_raw(rho, v1, v2, v3, p):
    en = p * (1.0 / GAMMA_LESS) + 0.5 * rho * (v1 * v1 + v2 * v2 + v3 * v3)
    return (rho, rho * v1, rho * v2, rho * v3, en), (v1, v2, v3, p, jnp.sqrt(1.4 * p / rho))


def flux(state, prim, d):
    rho, m1, m2, m3, en = state
    v, p = prim[d], prim[3]
    out = [state[1 + d], m1 * v, m2 * v, m3 * v, (en + p) * v]
    out[1 + d] = out[1 + d] + p
    return out


def add_direction(acc, here, prim, up, uprim, down, dprim, d):
    fu, fd = flux(up, uprim, d), flux(down, dprim, d)
    s0 = jnp.abs(prim[d]) + prim[4]
    lu = jnp.maximum(s0, jnp.abs(uprim[d]) + uprim[4])
    ld = jnp.maximum(s0, jnp.abs(dprim[d]) + dprim[4])
    out = []
    for c in range(5):
        term = (fu[c] - fd[c]) - lu * (up[c] - here[c]) + ld * (here[c] - down[c])
        out.append(term if acc is None else acc[c] + term)
    return out


def bulk_kernel(rho_ref, vel_ref, pre_ref, xlo_ref, xhi_ref, ylo_ref, yhi_ref, out_ref, ua, pa, ub, pb):
    lane = lax.broadcasted_iota(jnp.int32, (8, 128), 1)
    first, last = lane == 0, lane == 127

    def put(planes, rows, raw):
        state, prim = from_raw(*raw)
        for c in range(5):
            ua[c, planes, rows, :] = state[c]
            pa[c, planes, rows, :] = prim[c]

    def own(i, _):
        for r in range(0, 64, 8):
            rows = pl.ds(r, 8)
            put(i + 2, pl.ds(r + YOFF, 8), (rho_ref[i, rows, :], vel_ref[0, i, rows, :], vel_ref[1, i, rows, :], vel_ref[2, i, rows, :], pre_ref[i, rows, :]))
        put(i + 2, pl.ds(YOFF - 2, 2), [ylo_ref[c, i] for c in range(5)])
        put(i + 2, pl.ds(YOFF + 64, 2), [yhi_ref[c, i] for c in range(5)])
        return 0

    lax.fori_loop(0, 4, own, 0)

    def halo(i, _):
        for ref, base in ((xlo_ref, 0), (xhi_ref, 6)):
            for r in range(0, 64, 8):
                put(base + i, pl.ds(r + YOFF, 8), [ref[c, i, pl.ds(r, 8), :] for c in range(5)])
            put(base + i, pl.ds(YOFF + 64, 2), [ref[c, i, pl.ds(64, 2), :] for c in range(5)])
            put(base + i, pl.ds(YOFF - 2, 2), [ref[c, i, pl.ds(66, 2), :] for c in range(5)])
        return 0

    lax.fori_loop(0, 2, halo, 0)

    def update(u, q, i, r, n):
        def load(plane, row):
            rows = pl.ds(row, n)
            return [u[c, plane, rows, :] for c in range(5)], [q[c, plane, rows, :] for c in range(5)]

        here, prim = load(i, r)
        acc = None
        for d, (up, down) in enumerate((((i + 1, r), (i - 1, r)), ((i, r + 1), (i, r - 1)))):
            uu, uq = load(*up)
            du, dq = load(*down)
            acc = add_direction(acc, here, prim, uu, uq, du, dq, d)

        def shifted(x, sign, step, edge):
            return jnp.where(edge[:n], sign * x if sign < 0 else x, pltpu.roll(x, step, 1))

        signs = (1, 1, 1, -1, 1)
        qsigns = (None, None, -1, 1, 1)
        zu = [shifted(here[c], signs[c], 127, last) for c in range(5)]
        zd = [shifted(here[c], signs[c], 1, first) for c in range(5)]
        zuq = [None if qsigns[c] is None else shifted(prim[c], qsigns[c], 127, last) for c in range(5)]
        zdq = [None if qsigns[c] is None else shifted(prim[c], qsigns[c], 1, first) for c in range(5)]
        acc = add_direction(acc, here, prim, zu, zuq, zd, zdq, 2)
        return [here[c] - KFL * acc[c] for c in range(5)]

    def step_one(i, _):
        for r, n in [(YOFF - 8, 8)] + [(YOFF + k, 8) for k in range(0, 72, 8)]:
            if r == YOFF - 8:
                r, n = YOFF - 1, 1
            if r == YOFF + 64:
                n = 1
            new = update(ua, pa, i, r, n)
            prim = euler_prims(*new)
            for c in range(5):
                ub[c, i, pl.ds(r, n), :] = new[c]
                pb[c, i, pl.ds(r, n), :] = prim[c]
        return 0

    lax.fori_loop(1, 7, step_one, 0)

    def step_two(i, _):
        for r in range(0, 64, 8):
            new = update(ub, pb, i + 2, r + YOFF, 8)
            for c in range(5):
                out_ref[c, i, pl.ds(r, 8), :] = new[c]
        return 0

    lax.fori_loop(0, 4, step_two, 0)


def bulk_euler(density, velocity, pressure, xlo, xhi, ylo, yhi):
    vm = pl.BlockSpec(memory_space=pltpu.VMEM)
    return pl.pallas_call(
        bulk_kernel,
        out_shape=jax.ShapeDtypeStruct((5, 4, 64, 128), jnp.float32),
        in_specs=[vm] * 7,
        out_specs=vm,
        scratch_shapes=[pltpu.VMEM((5, 8, YROWS, 128), jnp.float32)] * 4,
        compiler_params=pltpu.CompilerParams(vmem_limit_bytes=32 * 1024 * 1024),
        cost_estimate=pl.CostEstimate(flops=60_000_000, bytes_accessed=3_000_000, transcendentals=100_000),
        name="bulk_euler",
    )(density, velocity, pressure, xlo, xhi, ylo, yhi)


def pressure_of(fields):
    kinetic = (
        0.5 * (fields[1] * fields[1] + fields[2] * fields[2] + fields[3] * fields[3]) / fields[0]
    )
    return GAMMA_LESS * (fields[4] - kinetic)


def laplace(field):
    return (
        field[2:, 1:-1]
        + field[:-2, 1:-1]
        + field[1:-1, 2:]
        + field[1:-1, :-2]
        - 4.0 * field[1:-1, 1:-1]
    )


def pick_rows(selector, table):
    return jnp.dot(selector, table, precision=lax.Precision.HIGHEST)


def body(
    density,
    velocity,
    pressure,
    deck_disp,
    deck_prev,
    stay_stiff,
    stay_tension,
    anchor_node,
    failed_stay,
    facet_cells,
    facet_owner,
    facet_row,
    facet_count,
):
    raw = jnp.concatenate([density[None], velocity, pressure[None]], axis=0)
    around = [(i, (i + 1) % 4) for i in range(4)]
    back = [(i, (i - 1) % 4) for i in range(4)]
    ylo = lax.ppermute(raw[:, :, 62:], "sect", around)
    yhi = lax.ppermute(raw[:, :, :2], "sect", back)
    wide = jnp.concatenate([raw, yhi, ylo, jnp.ones((5, 4, 4, 128), jnp.float32)], axis=2)
    count = lax.axis_size("fluid")
    xlo = lax.ppermute(wide[:, 2:], "fluid", [(i, (i + 1) % count) for i in range(count)])
    xhi = lax.ppermute(wide[:, :2], "fluid", [(i, (i - 1) % count) for i in range(count)])
    fields = bulk_euler(density, velocity, pressure, xlo, xhi, ylo, yhi)
    pressure_flat = pressure_of(fields[:, :, :, 0]).reshape(-1)
    cell_ids = jnp.arange(pressure_flat.shape[0], dtype=jnp.int32)
    slot_count, block_width = facet_cells.shape
    fluid_count = lax.axis_size("fluid")
    capacity = slot_count // fluid_count

    def sample_group(group_cells):
        flat_ids = group_cells.reshape(-1)
        picker = (flat_ids[:, None] == cell_ids[None, :]).astype(jnp.float32)
        return pick_rows(picker, pressure_flat).reshape(group_cells.shape)

    grouped = facet_cells.reshape(slot_count // SLOT_GROUP, SLOT_GROUP, block_width)
    samples = lax.map(sample_group, grouped).reshape(slot_count, block_width)
    alive_slot = jnp.arange(slot_count, dtype=jnp.int32) < facet_count[0]
    values = jnp.where(alive_slot[:, None], samples - AMBIENT, jnp.zeros_like(samples))
    owners = facet_owner[:, 0]
    matches = (owners[:, None] == jnp.arange(fluid_count, dtype=jnp.int32)[None, :]).astype(
        jnp.int32
    )
    earlier = jnp.cumsum(matches, axis=0) - matches
    within = jnp.sum(earlier * matches, axis=1)
    position = owners * capacity + within
    placement = (position[:, None] == jnp.arange(slot_count, dtype=jnp.int32)[None, :]).astype(
        jnp.float32
    )
    packed = pick_rows(placement.T, values).reshape(fluid_count, capacity, block_width)
    row_packed = pick_rows(placement.T, facet_row.astype(jnp.float32)).reshape(
        fluid_count, capacity, 1
    )
    got_values, got_rows = (
        lax.all_to_all(packed, "fluid", split_axis=0, concat_axis=0, tiled=True),
        lax.all_to_all(row_packed, "fluid", split_axis=0, concat_axis=0, tiled=True),
    )
    rows_tile, width_tile = deck_disp.shape
    got_index = got_rows.reshape(-1).astype(jnp.int32)
    selector_rows = (got_index[:, None] == jnp.arange(rows_tile, dtype=jnp.int32)[None, :]).astype(
        jnp.float32
    )
    deck_load = pick_rows(selector_rows.T, got_values.reshape(-1, block_width))
    fluid_index = lax.axis_index("fluid")
    sect_index = lax.axis_index("sect")
    deck_width = width_tile * lax.axis_size("sect")
    anchor_row = anchor_node // deck_width
    anchor_col = anchor_node % deck_width
    inside = (anchor_row // rows_tile == fluid_index) & (anchor_col // width_tile == sect_index)
    local_node = (anchor_row - fluid_index * rows_tile) * width_tile + (
        anchor_col - sect_index * width_tile
    )
    node_ids = jnp.arange(rows_tile * width_tile, dtype=jnp.int32)
    selector_stay = ((local_node[:, None] == node_ids[None, :]) & inside[:, None]).astype(
        jnp.float32
    )
    alive_stay = (jnp.arange(stay_stiff.shape[0], dtype=jnp.int32) != failed_stay[0]).astype(
        jnp.float32
    )
    current = deck_disp
    previous = deck_prev
    for substep in range(SSTEPS):
        padded_deck = with_halo(current, (("fluid", 0), ("sect", 1)), 2, False)
        bending = laplace(laplace(padded_deck))
        anchored = pick_rows(selector_stay, current.reshape(-1))
        stay_force = alive_stay * (stay_tension - stay_stiff * anchored)
        force_field = pick_rows(stay_force, selector_stay).reshape(rows_tile, width_tile)
        following = 2.0 * current - previous + STEP_DECK * (deck_load + force_field - bending)
        previous = current
        current = following
    outgoing = pick_rows(selector_rows, current).reshape(fluid_count, capacity, block_width)
    incoming = lax.all_to_all(outgoing, "fluid", split_axis=0, concat_axis=0, tiled=True)
    returned = pick_rows(placement, incoming.reshape(slot_count, block_width))
    facet_disp = jnp.where(alive_slot[:, None], returned, jnp.zeros_like(returned))
    return (fields, current, facet_disp)


def solution(mesh):
    return jax.shard_map(
        body,
        mesh=mesh,
        in_specs=(
            P("fluid", "sect", None),
            P(None, "fluid", "sect", None),
            P("fluid", "sect", None),
            P("fluid", "sect"),
            P("fluid", "sect"),
            P(),
            P(),
            P(),
            P(),
            P(("fluid", "sect"), None),
            P(("fluid", "sect"), None),
            P(("fluid", "sect")),
            P(("fluid", "sect")),
        ),
        out_specs=(P(None, "fluid", "sect", None), P("fluid", "sect"), P(("fluid", "sect"), None)),
        check_vma=False,
    )
```

```python
import jax
import jax.numpy as jnp
from jax import lax
from jax.experimental import pallas as pl
from jax.experimental.pallas import tpu as pltpu
from jax.sharding import PartitionSpec as P

STEP_FLUID = 0.045
STEP_DECK = 0.06
GAMMA_LESS = 0.4
AMBIENT = 1.0

THIN = 0
TABLE = 64
DECK = 72
EDGES = 88
NT = (((1,), (1,)), ((), ()))
NN = (((1,), (0,)), ((), ()))


def vmem(count):
    return [pl.BlockSpec(memory_space=pltpu.VMEM)] * count


def local_call(kernel, shapes, name, args, scratch=(), flops=1_000_000, smem=()):
    single = not isinstance(shapes, list)
    outs = [s if isinstance(s, jax.ShapeDtypeStruct) else jax.ShapeDtypeStruct(s, jnp.float32) for s in ([shapes] if single else shapes)]
    specs = [pl.BlockSpec(memory_space=pltpu.SMEM if i in smem else pltpu.VMEM) for i in range(len(args))]
    result = pl.pallas_call(
        kernel,
        out_shape=outs,
        in_specs=specs,
        out_specs=vmem(len(outs)),
        scratch_shapes=list(scratch),
        compiler_params=pltpu.CompilerParams(vmem_limit_bytes=32 * 1024 * 1024),
        cost_estimate=pl.CostEstimate(flops=flops, bytes_accessed=1_000_000, transcendentals=0),
        name=name,
    )(*args)
    return result[0] if single else result


def iota(shape, axis):
    return lax.broadcasted_iota(jnp.int32, shape, axis)


def split3(x):
    high = x.astype(jnp.bfloat16)
    rest = x - high.astype(jnp.float32)
    middle = rest.astype(jnp.bfloat16)
    low = (rest - middle.astype(jnp.float32)).astype(jnp.bfloat16)
    return high, middle, low


def pick(onehot, table, dims=NN):
    onehot = onehot.astype(jnp.float32).astype(jnp.bfloat16)
    total = None
    for part in split3(table):
        term = lax.dot_general(onehot, part, dims, preferred_element_type=jnp.float32)
        total = term if total is None else total + term
    return total


def side_rows():
    sect = lax.axis_index("sect")
    left, right = lax.rem(sect + 3, 4), lax.rem(sect + 1, 4)
    return pl.multiple_of(left * 128, 128), pl.multiple_of(right * 128, 128)


YOFF = 8
YROWS = 80
KFL = 0.5 * STEP_FLUID


def euler_prims(rho, m1, m2, m3, en):
    inv = 1.0 / rho
    v1, v2, v3 = m1 * inv, m2 * inv, m3 * inv
    p = GAMMA_LESS * (en - 0.5 * (m1 * v1 + m2 * v2 + m3 * v3))
    return v1, v2, v3, p, jnp.sqrt(1.4 * p * inv)


def from_raw(rho, v1, v2, v3, p):
    en = p * (1.0 / GAMMA_LESS) + 0.5 * rho * (v1 * v1 + v2 * v2 + v3 * v3)
    return (rho, rho * v1, rho * v2, rho * v3, en), (v1, v2, v3, p, jnp.sqrt(1.4 * p / rho))


def flux(state, prim, d):
    rho, m1, m2, m3, en = state
    v, p = prim[d], prim[3]
    out = [state[1 + d], m1 * v, m2 * v, m3 * v, (en + p) * v]
    out[1 + d] = out[1 + d] + p
    return out


def add_direction(acc, here, prim, up, uprim, down, dprim, d):
    fu, fd = flux(up, uprim, d), flux(down, dprim, d)
    s0 = jnp.abs(prim[d]) + prim[4]
    lu = jnp.maximum(s0, jnp.abs(uprim[d]) + uprim[4])
    ld = jnp.maximum(s0, jnp.abs(dprim[d]) + dprim[4])
    out = []
    for c in range(5):
        term = (fu[c] - fd[c]) - lu * (up[c] - here[c]) + ld * (here[c] - down[c])
        out.append(term if acc is None else acc[c] + term)
    return out


def prep_kernel(rho_ref, vel_ref, pre_ref, w_ref, u_ref, ext_ref, cor_ref, own_ref, edge_ref):
    core = lax.axis_index("fluid") % 2
    chooser = iota((16, 128), 0) == iota((16, 128), 1)
    raw = [rho_ref, vel_ref.at[0], vel_ref.at[1], vel_ref.at[2], pre_ref]
    own_ref[15:16, :] = jnp.zeros((1, 256), jnp.float32)
    for c in range(5):
        own_ref[3 * c : 3 * c + 3, :] = pick(chooser, raw[c][...].reshape(256, 128), NT)[0:3]
        for side, y in ((0, 0), (1, 62)):
            for i in range(4):
                edge_ref[pl.ds(40 * side + 8 * c + 2 * i, 2), :] = raw[c][i, pl.ds(y, 2), :]
    first, last = own_ref[:, 0:128], own_ref[:, 128:256]
    even = core == 0
    ext_ref[0:16, :] = jnp.where(even, first, last)
    cor_ref[0:16, :] = jnp.where(even, last, first)
    wf, wl, uf, ul = w_ref[0:4, :], w_ref[60:64, :], u_ref[0:2, :], u_ref[62:64, :]
    ext_ref[16:20, :] = jnp.where(even, wf, wl)
    cor_ref[16:20, :] = jnp.where(even, wl, wf)
    ext_ref[20:22, :] = jnp.where(even, uf, ul)
    cor_ref[20:22, :] = jnp.where(even, ul, uf)
    ext_ref[22:24, :] = jnp.zeros((2, 128), jnp.float32)
    cor_ref[22:24, :] = jnp.zeros((2, 128), jnp.float32)


def table_kernel(cells_ref, owner_ref, row_ref, count_ref, tab_ref, pos_ref, place_ref):
    owner = jnp.broadcast_to(owner_ref[...].astype(jnp.float32), (128, 128))
    owner_row = owner.T
    same = owner == owner_row
    down, along = iota((128, 128), 0), iota((128, 128), 1)
    within = jnp.sum(jnp.where(same & (along < down), 1.0, 0.0), axis=1, keepdims=True)
    within_row = jnp.sum(jnp.where(same & (down < along), 1.0, 0.0), axis=0, keepdims=True)
    position = (2.0 * owner[:, 0:1] + within).astype(jnp.int32)
    pos_ref[...] = jnp.broadcast_to(2.0 * owner_row[0:1, :] + within_row, (8, 128))
    place = jnp.where(position == along, 1.0, 0.0).astype(jnp.bfloat16)
    place_ref[...] = place
    r, c = iota((16, 128), 0), iota((16, 128), 1)
    columns = jnp.where(((r < 2) & (c == r)) | ((r >= 2) & (r < 4) & (c == r + 124)), 1.0, 0.0).astype(jnp.bfloat16)
    cells = cells_ref[...].astype(jnp.float32).astype(jnp.bfloat16)
    picked = lax.dot_general(columns, cells, NT, preferred_element_type=jnp.float32)
    live = iota((1, 128), 1) < count_ref[0]
    code = jnp.where(live, row_ref[...] + 128, 0).astype(jnp.float32)
    stacked = jnp.where(r == 4, jnp.broadcast_to(code, (16, 128)), picked).astype(jnp.bfloat16)
    tab_ref[...] = lax.dot_general(stacked, place, NN, preferred_element_type=jnp.float32)[0:8]


def middle_kernel(ext_ref, cor_ref, own_ref, w_ref, u_ref, tab_ref, edge_ref, out_ref, deck_ref, wide):
    fluid, sect = lax.axis_index("fluid"), lax.axis_index("sect")
    even = fluid % 2 == 0
    ext, cor = ext_ref[...], cor_ref[...]
    low, high = jnp.where(even, ext, cor), jnp.where(even, cor, ext)
    low_deck = jnp.where(fluid == 0, 0.0, low[16:24])
    high_deck = jnp.where(fluid == 63, 0.0, high[16:24])
    wide[...] = jnp.zeros((2, 128, 128), jnp.float32)
    wide[0, 0:4, :] = low_deck[0:4]
    wide[0, 4:68, :] = w_ref[...]
    wide[0, 68:72, :] = high_deck[0:4]
    wide[1, 2:4, :] = low_deck[4:6]
    wide[1, 4:68, :] = u_ref[...]
    wide[1, 68:70, :] = high_deck[4:6]
    deck_ref[...] = wide[:, 0:72, :]
    w_columns, u_columns = wide[0].T, wide[1].T
    pieces = [low[0:16], own_ref[:, 0:128], own_ref[:, 128:256], high[0:16], tab_ref[...], w_columns[0:4], w_columns[124:128], u_columns[0:2], u_columns[126:128], jnp.zeros((4, 128), jnp.float32)]
    block = jnp.concatenate(pieces, axis=0)
    for t in range(4):
        out_ref[t, 0:EDGES, :] = block
        out_ref[t, EDGES:128, :] = edge_ref[0:40, :]
    out_ref[lax.rem(sect + 1, 4), EDGES:128, :] = edge_ref[40:80, :]


def wall_press(around_ref):
    lane = iota((8, 128), 1)
    low_half, y = lane < 64, lane & 63

    def get(t, c, z):
        part = around_ref[pl.ds(THIN + 16 * t + 3 * c + z, 4, stride=128), :]
        return jnp.concatenate([part, part], axis=0)

    def x_around(tiles):
        turned = [pltpu.roll(x, 64, 1) for x in tiles]
        after, before = turned[1:] + turned[-1:], turned[:1] + turned[:-1]
        ups = [jnp.where(low_half, a, b) for a, b in zip(turned, after)]
        downs = [jnp.where(low_half, b, a) for a, b in zip(turned, before)]
        return ups, downs

    def y_up(x):
        return jnp.where(y == 63, pltpu.roll(pltpu.roll(x, 7, 0), 63, 1), pltpu.roll(x, 127, 1))

    def y_down(x):
        return jnp.where(y == 0, pltpu.roll(pltpu.roll(x, 1, 0), 65, 1), pltpu.roll(x, 1, 1))

    def mirrored(state, prim):
        return [state[0], state[1], state[2], -state[3], state[4]], [prim[0], prim[1], -prim[2], prim[3], prim[4]]

    def advance(states, prims, layer, tiles):
        here, q = states[layer], prims[layer]
        xu = [x_around([here[t][c] for t in range(4)]) for c in range(5)]
        xq = {c: x_around([q[t][c] for t in range(4)]) for c in (0, 3, 4)}
        result = []
        for t in tiles:
            pack = [None] * 5
            up, down = [xu[c][0][t] for c in range(5)], [xu[c][1][t] for c in range(5)]
            upq, downq = list(pack), list(pack)
            for c in (0, 3, 4):
                upq[c], downq[c] = xq[c][0][t], xq[c][1][t]
            acc = add_direction(None, here[t], q[t], up, upq, down, downq, 0)
            up, down = [y_up(here[t][c]) for c in range(5)], [y_down(here[t][c]) for c in range(5)]
            upq, downq = list(pack), list(pack)
            for c in (1, 3, 4):
                upq[c], downq[c] = y_up(q[t][c]), y_down(q[t][c])
            acc = add_direction(acc, here[t], q[t], up, upq, down, downq, 1)
            down, downq = mirrored(here[t], q[t]) if layer == 0 else (states[layer - 1][t], prims[layer - 1][t])
            acc = add_direction(acc, here[t], q[t], states[layer + 1][t], prims[layer + 1][t], down, downq, 2)
            result.append([here[t][c] - KFL * acc[c] for c in range(5)])
        return result

    states, prims = [], []
    for z in range(3):
        both = [from_raw(*[get(t, c, z) for c in range(5)]) for t in range(4)]
        states.append([b[0] for b in both])
        prims.append([b[1] for b in both])
    after = [advance(states, prims, z, range(4)) for z in range(2)]
    after_prims = [[euler_prims(*after[z][t]) for t in range(4)] for z in range(2)]
    final = advance(after, after_prims, 0, (1, 2))
    return [euler_prims(*final[i])[3] for i in range(2)]


def gather_lanes(tables, cells):
    index = cells & 127
    low = jnp.take_along_axis(jnp.broadcast_to(tables[0], cells.shape), index, axis=1, mode="promise_in_bounds")
    high = jnp.take_along_axis(jnp.broadcast_to(tables[1], cells.shape), index, axis=1, mode="promise_in_bounds")
    return jnp.where(cells < 128, low, high) - AMBIENT


def facet_kernel(around_ref, cells_ref, tab_ref, pos_ref, out_ref, press):
    fluid, sect = lax.axis_index("fluid"), lax.axis_index("sect")
    left, right = side_rows()
    first, second = wall_press(around_ref)
    press[0:8, :] = first
    press[8:16, :] = second

    def tables(s):
        return press[pl.ds(s, 1), :], press[pl.ds(s + 8, 1), :]

    values = gather_lanes(tables(sect), cells_ref[...])
    r = iota((512, 128), 0)
    wanted = 2 * (r >> 3) + (r & 7) - 2
    chooser = (pos_ref[0:1, :].astype(jnp.int32) == wanted) & ((r & 7) < 6)
    out_ref[...] = pick(chooser, values)
    left_tab = around_ref[pl.ds(left + TABLE, 8), :]
    right_tab = around_ref[pl.ds(right + TABLE, 8), :]
    left_values = gather_lanes(tables(lax.rem(sect + 3, 4)), left_tab.astype(jnp.int32))
    right_values = gather_lanes(tables(lax.rem(sect + 1, 4)), right_tab.astype(jnp.int32))
    left_code = jnp.where(sect == 0, 0.0, left_tab[4:5])
    right_code = jnp.where(sect == 3, 0.0, right_tab[4:5])
    rows = [tab_ref[4:5, :], left_code, left_values[2:3], left_values[3:4], right_code, right_values[0:1], right_values[1:2]]
    spread = jnp.concatenate([jnp.broadcast_to(x, (8, 128)) for x in rows] + [jnp.zeros((72, 128), jnp.float32)], axis=0)
    place = iota((128, 128), 0) & 7
    weights = jnp.concatenate([jnp.where(place == 2, spread, 0.0), jnp.where(place == 3, spread, 0.0)], axis=1)
    o, p = iota((64, 256), 0), iota((64, 256), 1)
    base = pick(2 * o + (p >> 7) == (p & 127), weights, NT)
    owner = iota((64, 128), 0)
    before = jnp.where(owner == 0, 0.0, pltpu.roll(base, 1, 0))
    after = jnp.where(owner == 63, 0.0, pltpu.roll(base, 63, 0))
    meta = base + pltpu.roll(before, 126, 1) + pltpu.roll(after, 2, 1)
    out_ref[pl.ds(7, 64, stride=8), :] = meta


def bending_of(w):
    def laplace(x):
        rows, lanes = x.shape
        return pltpu.roll(x, 1, 0) + pltpu.roll(x, rows - 1, 0) + pltpu.roll(x, 1, 1) + pltpu.roll(x, lanes - 1, 1) - 4.0 * x

    return laplace(laplace(w))


def early_kernel(around_ref, deck_ref, stiff_ref, tension_ref, anchor_ref, failed_ref, out_ref, turn):
    fluid, sect = lax.axis_index("fluid"), lax.axis_index("sect")
    left, right = side_rows()
    turn[...] = jnp.zeros((2, 128, 128), jnp.float32)
    turn[0, 0:4, :] = jnp.where(sect == 3, 0.0, around_ref[pl.ds(right + DECK, 4), :])
    turn[0, 124:128, :] = jnp.where(sect == 0, 0.0, around_ref[pl.ds(left + DECK + 4, 4), :])
    turn[1, 0:2, :] = jnp.where(sect == 3, 0.0, around_ref[pl.ds(right + DECK + 8, 2), :])
    turn[1, 126:128, :] = jnp.where(sect == 0, 0.0, around_ref[pl.ds(left + DECK + 10, 2), :])
    w = jnp.concatenate([deck_ref[0], turn[0].T[0:72]], axis=1)
    u = jnp.concatenate([deck_ref[1], turn[1].T[0:72]], axis=1)
    anchor = anchor_ref[...]
    count = anchor.shape[1]
    alive = iota((1, count), 1) != failed_ref[0]
    row = (anchor >> 9) - 64 * fluid + 4
    column = (anchor & 511) - 128 * sect
    lane = jnp.where((column >= -4) & (column < 132) & alive, column & 255, -1)
    rows = iota((72, count), 0) == row
    columns = iota((256, count), 0) == lane
    alpha = pick(rows, jnp.where(columns, stiff_ref[...], 0.0), NT)
    beta = pick(rows, jnp.where(columns, tension_ref[...], 0.0), NT)
    first = 2.0 * w - u + STEP_DECK * (beta - alpha * w - bending_of(w))
    r, c = iota((72, 256), 0) - 4 + 64 * fluid, iota((72, 256), 1)
    c = jnp.where(c < 132, c, c - 256) + 128 * sect
    inside = (r >= 0) & (r < 4096) & (c >= 0) & (c < 512) & (c >= 128 * sect - 4)
    out_ref[0] = w
    out_ref[1] = jnp.where(inside, first, 0.0)
    out_ref[2] = alpha
    out_ref[3] = beta


def deck_kernel(got_ref, early_ref, deck_ref, ret_ref, spread):
    meta = got_ref[pl.ds(7, 64, stride=8), :]
    for j in range(8):
        spread[pl.ds(j, 64, stride=8), :] = meta
    r, c = iota((512, 128), 0), iota((512, 128), 1)
    own = jnp.where((c & 7) == (r & 7), spread[...], 0.0)
    kinds = pick((iota((16, 128), 1) >> 3) == iota((16, 128), 0), own, NT)
    k = iota((1, 512), 1)
    offset = 64 * ((k & 7) >> 1) - 64 + 4 - 128

    def rows_of(kind):
        code = kinds[kind : kind + 1].astype(jnp.int32)
        local = jnp.where((code > 0) & ((k & 7) < 6), code + offset, -1)
        return iota((72, 512), 0) == local

    centre = pick(rows_of(0), got_ref[...])
    lanes = iota((128, 512), 0)
    from_left = jnp.where(lanes == 126, kinds[2:3], jnp.where(lanes == 127, kinds[3:4], 0.0))
    from_right = jnp.where(lanes == 0, kinds[5:6], jnp.where(lanes == 1, kinds[6:7], 0.0))
    sides = pick(rows_of(1), from_left, NT) + pick(rows_of(4), from_right, NT)
    load = jnp.concatenate([centre, sides], axis=1)
    first = early_ref[1] + STEP_DECK * load
    second = 2.0 * first - early_ref[0] + STEP_DECK * (load + early_ref[3] - early_ref[2] * first - bending_of(first))
    tile = second[4:68, 0:128]
    deck_ref[...] = tile
    for i in range(2):
        row = meta[:, 2 + i : 3 + i].astype(jnp.int32) - 128
        ret_ref[:, i, :] = pick(iota((64, 64), 1) == row, tile)


def final_kernel(got_ref, place_ref, out_ref):
    out_ref[...] = pick(place_ref[...], got_ref[...])


def pack_kernel(rho_ref, vel_ref, pre_ref, around_ref, ext_ref, cor_ref):
    core = lax.axis_index("fluid") % 2
    left, right = side_rows()
    raw = [rho_ref, vel_ref.at[0], vel_ref.at[1], vel_ref.at[2], pre_ref]
    for ref, start in ((ext_ref, 2 * core), (cor_ref, 2 - 2 * core)):
        for c in range(5):
            for i in range(2):
                ref[c, i, 0:64, :] = raw[c][start + i]
                ref[c, i, 64:66, :] = around_ref[pl.ds(right + EDGES + 8 * c + 2 * (start + i), 2), :]
                ref[c, i, 66:68, :] = around_ref[pl.ds(left + EDGES + 8 * c + 2 * (start + i), 2), :]
                ref[c, i, 68:72, :] = jnp.ones((4, 128), jnp.float32)


def bulk_kernel(rho_ref, vel_ref, pre_ref, ext_ref, cor_ref, around_ref, out_ref, ua, pa, ub, pb):
    core = lax.axis_index("fluid") % 2
    left, right = side_rows()
    lane = lax.broadcasted_iota(jnp.int32, (8, 128), 1)
    first, last = lane == 0, lane == 127

    def put(planes, rows, raw):
        state, prim = from_raw(*raw)
        for c in range(5):
            ua[c, planes, rows, :] = state[c]
            pa[c, planes, rows, :] = prim[c]

    def own(i, _):
        for r in range(0, 64, 8):
            rows = pl.ds(r, 8)
            put(i + 2, pl.ds(r + YOFF, 8), (rho_ref[i, rows, :], vel_ref[0, i, rows, :], vel_ref[1, i, rows, :], vel_ref[2, i, rows, :], pre_ref[i, rows, :]))
        put(i + 2, pl.ds(YOFF - 2, 2), [around_ref[pl.ds(left + EDGES + 8 * c + 2 * i, 2), :] for c in range(5)])
        put(i + 2, pl.ds(YOFF + 64, 2), [around_ref[pl.ds(right + EDGES + 8 * c + 2 * i, 2), :] for c in range(5)])
        return 0

    lax.fori_loop(0, 4, own, 0)

    def halo(i, _):
        for ref, base in ((ext_ref, 6 * core), (cor_ref, 6 - 6 * core)):
            for r in range(0, 64, 8):
                put(base + i, pl.ds(r + YOFF, 8), [ref[c, i, pl.ds(r, 8), :] for c in range(5)])
            put(base + i, pl.ds(YOFF + 64, 2), [ref[c, i, pl.ds(64, 2), :] for c in range(5)])
            put(base + i, pl.ds(YOFF - 2, 2), [ref[c, i, pl.ds(66, 2), :] for c in range(5)])
        return 0

    lax.fori_loop(0, 2, halo, 0)

    def update(u, q, i, r, n):
        def load(plane, row):
            rows = pl.ds(row, n)
            return [u[c, plane, rows, :] for c in range(5)], [q[c, plane, rows, :] for c in range(5)]

        here, prim = load(i, r)
        acc = None
        for d, (up, down) in enumerate((((i + 1, r), (i - 1, r)), ((i, r + 1), (i, r - 1)))):
            uu, uq = load(*up)
            du, dq = load(*down)
            acc = add_direction(acc, here, prim, uu, uq, du, dq, d)

        def shifted(x, sign, step, edge):
            return jnp.where(edge[:n], sign * x if sign < 0 else x, pltpu.roll(x, step, 1))

        signs = (1, 1, 1, -1, 1)
        qsigns = (None, None, -1, 1, 1)
        zu = [shifted(here[c], signs[c], 127, last) for c in range(5)]
        zd = [shifted(here[c], signs[c], 1, first) for c in range(5)]
        zuq = [None if qsigns[c] is None else shifted(prim[c], qsigns[c], 127, last) for c in range(5)]
        zdq = [None if qsigns[c] is None else shifted(prim[c], qsigns[c], 1, first) for c in range(5)]
        acc = add_direction(acc, here, prim, zu, zuq, zd, zdq, 2)
        return [here[c] - KFL * acc[c] for c in range(5)]

    def step_one(i, _):
        for r, n in [(YOFF - 8, 8)] + [(YOFF + k, 8) for k in range(0, 72, 8)]:
            if r == YOFF - 8:
                r, n = YOFF - 1, 1
            if r == YOFF + 64:
                n = 1
            new = update(ua, pa, i, r, n)
            prim = euler_prims(*new)
            for c in range(5):
                ub[c, i, pl.ds(r, n), :] = new[c]
                pb[c, i, pl.ds(r, n), :] = prim[c]
        return 0

    lax.fori_loop(1, 7, step_one, 0)

    def step_two(i, _):
        for r in range(0, 64, 8):
            new = update(ub, pb, i + 2, r + YOFF, 8)
            for c in range(5):
                out_ref[c, i, pl.ds(r, 8), :] = new[c]
        return 0

    lax.fori_loop(0, 4, step_two, 0)


def bulk_euler(density, velocity, pressure, ext, cor, around):
    return local_call(
        bulk_kernel,
        (5, 4, 64, 128),
        "bulk_euler",
        (density, velocity, pressure, ext, cor, around),
        scratch=[pltpu.VMEM((5, 8, YROWS, 128), jnp.float32)] * 4,
        flops=60_000_000,
    )


def body(
    density,
    velocity,
    pressure,
    deck_disp,
    deck_prev,
    stay_stiff,
    stay_tension,
    anchor_node,
    failed_stay,
    facet_cells,
    facet_owner,
    facet_row,
    facet_count,
):
    count = lax.axis_size("fluid")
    outward = [(i, (i + 1) % count if i % 2 else (i - 1) % count) for i in range(count)]
    inward = [(i, i ^ 1) for i in range(count)]
    ext, cor, own, edge = local_call(
        prep_kernel, [(24, 128), (24, 128), (16, 256), (80, 128)], "prep", (density, velocity, pressure, deck_disp, deck_prev)
    )
    ext = lax.ppermute(ext, "fluid", outward)
    cor = lax.ppermute(cor, "fluid", inward)
    tab, pos, place = local_call(
        table_kernel,
        [(8, 128), (8, 128), jax.ShapeDtypeStruct((128, 128), jnp.bfloat16)],
        "tables",
        (facet_cells, facet_owner, facet_row.reshape(1, -1), facet_count),
        smem=(3,),
    )
    block, deck = local_call(
        middle_kernel,
        [(4, 128, 128), (2, 72, 128)],
        "middle",
        (ext, cor, own, deck_disp, deck_prev, tab, edge),
        scratch=[pltpu.VMEM((2, 128, 128), jnp.float32)],
    )
    around = lax.all_to_all(block, "sect", split_axis=0, concat_axis=0, tiled=True).reshape(512, 128)
    facets = local_call(
        facet_kernel, (512, 128), "facets", (around, facet_cells, tab, pos), scratch=[pltpu.VMEM((16, 128), jnp.float32)], flops=4_000_000
    )
    got = lax.all_to_all(facets.reshape(64, 8, 128), "fluid", split_axis=0, concat_axis=0, tiled=True).reshape(512, 128)
    early = local_call(
        early_kernel,
        (4, 72, 256),
        "early_deck",
        (around, deck, stay_stiff.reshape(1, -1), stay_tension.reshape(1, -1), anchor_node.reshape(1, -1), failed_stay),
        scratch=[pltpu.VMEM((2, 128, 128), jnp.float32)],
        smem=(5,),
    )
    ext_planes, cor_planes = local_call(pack_kernel, [(5, 2, 72, 128), (5, 2, 72, 128)], "pack", (density, velocity, pressure, around))
    ext_planes = lax.ppermute(ext_planes, "fluid", outward)
    cor_planes = lax.ppermute(cor_planes, "fluid", inward)
    fields = bulk_euler(density, velocity, pressure, ext_planes, cor_planes, around)
    deck_next, back = local_call(
        deck_kernel, [(64, 128), (64, 2, 128)], "deck", (got, early), scratch=[pltpu.VMEM((512, 128), jnp.float32)], flops=4_000_000
    )
    back = lax.all_to_all(back, "fluid", split_axis=0, concat_axis=0, tiled=True)
    facet_disp = local_call(final_kernel, (128, 128), "final", (back.reshape(128, 128), place))
    return (fields, deck_next, facet_disp)


def solution(mesh):
    return jax.shard_map(
        body,
        mesh=mesh,
        in_specs=(
            P("fluid", "sect", None),
            P(None, "fluid", "sect", None),
            P("fluid", "sect", None),
            P("fluid", "sect"),
            P("fluid", "sect"),
            P(),
            P(),
            P(),
            P(),
            P(("fluid", "sect"), None),
            P(("fluid", "sect"), None),
            P(("fluid", "sect")),
            P(("fluid", "sect")),
        ),
        out_specs=(P(None, "fluid", "sect", None), P("fluid", "sect"), P(("fluid", "sect"), None)),
        check_vma=False,
    )
```

```python
import jax
import jax.numpy as jnp
from jax import lax
from jax.experimental import pallas as pl
from jax.experimental.pallas import tpu as pltpu
from jax.sharding import PartitionSpec as P

STEP_FLUID = 0.045
STEP_DECK = 0.06
GAMMA_LESS = 0.4
AMBIENT = 1.0

THIN = 0
TABLE = 64
DECK = 72
EDGES = 88
PER = 7
VALUES = 64
NT = (((1,), (1,)), ((), ()))
NN = (((1,), (0,)), ((), ()))


def local_call(kernel, shapes, name, args, scratch=(), flops=1_000_000, smem=(), hbm=(), out_hbm=(), free=False):
    outs = [jax.ShapeDtypeStruct(*s) if free else pltpu.HBM(*s) if i in out_hbm else pltpu.VMEM(*s) for i, s in enumerate(shapes)]
    spaces = [pltpu.SMEM if i in smem else pltpu.HBM if i in hbm else pltpu.VMEM for i in range(len(args))]
    args = [pltpu.with_memory_space_constraint(a, pltpu.HBM) if i in hbm else a for i, a in enumerate(args)]
    return pl.pallas_call(
        kernel,
        out_shape=outs,
        in_specs=[pl.BlockSpec(memory_space=s) for s in spaces],
        out_specs=[pl.BlockSpec(memory_space=pltpu.HBM if i in out_hbm else pltpu.VMEM) for i in range(len(outs))],
        scratch_shapes=list(scratch),
        compiler_params=pltpu.CompilerParams(vmem_limit_bytes=32 * 1024 * 1024),
        cost_estimate=pl.CostEstimate(flops=flops, bytes_accessed=1_000_000, transcendentals=0),
        name=name,
    )(*args)


def floats(*shape):
    return shape, jnp.float32


def iota(shape, axis):
    return lax.broadcasted_iota(jnp.int32, shape, axis)


def split3(x):
    high = x.astype(jnp.bfloat16)
    rest = x - high.astype(jnp.float32)
    middle = rest.astype(jnp.bfloat16)
    low = (rest - middle.astype(jnp.float32)).astype(jnp.bfloat16)
    return high, middle, low


def pick(onehot, table, dims=NN):
    onehot = onehot.astype(jnp.float32).astype(jnp.bfloat16)
    total = None
    for part in split3(table):
        term = lax.dot_general(onehot, part, dims, preferred_element_type=jnp.float32)
        total = term if total is None else total + term
    return total


def side_rows():
    sect = lax.axis_index("sect")
    left, right = lax.rem(sect + 3, 4), lax.rem(sect + 1, 4)
    return pl.multiple_of(left * 128, 128), pl.multiple_of(right * 128, 128)


YOFF = 8
YROWS = 80
KFL = 0.5 * STEP_FLUID


def euler_prims(rho, m1, m2, m3, en):
    inv = 1.0 / rho
    v1, v2, v3 = m1 * inv, m2 * inv, m3 * inv
    p = GAMMA_LESS * (en - 0.5 * (m1 * v1 + m2 * v2 + m3 * v3))
    return v1, v2, v3, p, jnp.sqrt(1.4 * p * inv)


def from_raw(rho, v1, v2, v3, p):
    en = p * (1.0 / GAMMA_LESS) + 0.5 * rho * (v1 * v1 + v2 * v2 + v3 * v3)
    return (rho, rho * v1, rho * v2, rho * v3, en), (v1, v2, v3, p, jnp.sqrt(1.4 * p / rho))


def flux(state, prim, d):
    rho, m1, m2, m3, en = state
    v, p = prim[d], prim[3]
    out = [state[1 + d], m1 * v, m2 * v, m3 * v, (en + p) * v]
    out[1 + d] = out[1 + d] + p
    return out


def add_direction(acc, here, prim, up, uprim, down, dprim, d):
    fu, fd = flux(up, uprim, d), flux(down, dprim, d)
    s0 = jnp.abs(prim[d]) + prim[4]
    lu = jnp.maximum(s0, jnp.abs(uprim[d]) + uprim[4])
    ld = jnp.maximum(s0, jnp.abs(dprim[d]) + dprim[4])
    out = []
    for c in range(5):
        term = (fu[c] - fd[c]) - lu * (up[c] - here[c]) + ld * (here[c] - down[c])
        out.append(term if acc is None else acc[c] + term)
    return out


def prep_kernel(rho_hbm, vel_hbm, pre_hbm, w_hbm, u_hbm, raw_ref, wu_ref, ext_ref, cor_ref, own_ref, sems):
    core = lax.axis_index("fluid") % 2
    pairs = [
        (rho_hbm, raw_ref.at[0]),
        (vel_hbm, raw_ref.at[pl.ds(1, 3)]),
        (pre_hbm, raw_ref.at[4]),
        (w_hbm, wu_ref.at[0]),
        (u_hbm, wu_ref.at[1]),
    ]
    copies = [pltpu.make_async_copy(a, b, sems.at[i]) for i, (a, b) in enumerate(pairs)]
    for copy in copies:
        copy.start()
    chooser = iota((16, 128), 0) == iota((16, 128), 1)
    own_ref[15:16, :] = jnp.zeros((1, 256), jnp.float32)
    ext_ref[22:24, :] = jnp.zeros((2, 128), jnp.float32)
    cor_ref[22:24, :] = jnp.zeros((2, 128), jnp.float32)
    for copy in copies:
        copy.wait()
    for c in range(5):
        own_ref[3 * c : 3 * c + 3, :] = pick(chooser, raw_ref[c].reshape(256, 128), NT)[0:3]
    first, last = own_ref[:, 0:128], own_ref[:, 128:256]
    even = core == 0
    ext_ref[0:16, :] = jnp.where(even, first, last)
    cor_ref[0:16, :] = jnp.where(even, last, first)
    wf, wl, uf, ul = wu_ref[0, 0:4, :], wu_ref[0, 60:64, :], wu_ref[1, 0:2, :], wu_ref[1, 62:64, :]
    ext_ref[16:20, :] = jnp.where(even, wf, wl)
    cor_ref[16:20, :] = jnp.where(even, wl, wf)
    ext_ref[20:22, :] = jnp.where(even, uf, ul)
    cor_ref[20:22, :] = jnp.where(even, ul, uf)


def table_kernel(cells_hbm, owner_hbm, row_hbm, raw_ref, count_ref, tab_ref, pos_ref, place_ref, cells_ref, edge_ref, slots_ref, sems):
    pairs = [(cells_hbm, cells_ref), (owner_hbm, slots_ref.at[pl.ds(0, 1)]), (row_hbm, slots_ref.at[pl.ds(8, 1)])]
    copies = [pltpu.make_async_copy(a, b, sems.at[i]) for i, (a, b) in enumerate(pairs)]
    for copy in copies:
        copy.start()
    for c in range(5):
        for side, y in ((0, 0), (1, 62)):
            for i in range(4):
                edge_ref[pl.ds(40 * side + 8 * c + 2 * i, 2), :] = raw_ref[c, i, pl.ds(y, 2), :]
    for copy in copies:
        copy.wait()
    owner_row = jnp.broadcast_to(slots_ref[0:1, :].astype(jnp.float32), (128, 128))
    owner = owner_row.T
    same = owner == owner_row
    down, along = iota((128, 128), 0), iota((128, 128), 1)
    within = jnp.sum(jnp.where(same & (along < down), 1.0, 0.0), axis=1, keepdims=True)
    within_row = jnp.sum(jnp.where(same & (down < along), 1.0, 0.0), axis=0, keepdims=True)
    position = (2.0 * owner[:, 0:1] + within).astype(jnp.int32)
    pos_ref[...] = jnp.broadcast_to(2.0 * owner_row[0:1, :] + within_row, (8, 128))
    place = jnp.where(position == along, 1.0, 0.0).astype(jnp.bfloat16)
    place_ref[...] = place
    r, c = iota((16, 128), 0), iota((16, 128), 1)
    columns = jnp.where(((r < 2) & (c == r)) | ((r >= 2) & (r < 4) & (c == r + 124)), 1.0, 0.0).astype(jnp.bfloat16)
    cells = cells_ref[...].astype(jnp.float32).astype(jnp.bfloat16)
    picked = lax.dot_general(columns, cells, NT, preferred_element_type=jnp.float32)
    live = iota((1, 128), 1) < count_ref[0]
    code = jnp.where(live, slots_ref[8:9, :] + 128, 0).astype(jnp.float32)
    stacked = jnp.where(r == 4, jnp.broadcast_to(code, (16, 128)), picked).astype(jnp.bfloat16)
    tab_ref[...] = lax.dot_general(stacked, place, NN, preferred_element_type=jnp.float32)[0:8]


def middle_kernel(ext_ref, cor_ref, own_ref, wu_ref, tab_ref, edge_ref, out_ref, deck_ref, wide):
    fluid, sect = lax.axis_index("fluid"), lax.axis_index("sect")
    even = fluid % 2 == 0
    ext, cor = ext_ref[...], cor_ref[...]
    low, high = jnp.where(even, ext, cor), jnp.where(even, cor, ext)
    low_deck = jnp.where(fluid == 0, 0.0, low[16:24])
    high_deck = jnp.where(fluid == 63, 0.0, high[16:24])
    wide[...] = jnp.zeros((2, 128, 128), jnp.float32)
    wide[0, 4:8, :] = low_deck[0:4]
    wide[0, 8:72, :] = wu_ref[0]
    wide[0, 72:76, :] = high_deck[0:4]
    wide[1, 6:8, :] = low_deck[4:6]
    wide[1, 8:72, :] = wu_ref[1]
    wide[1, 72:74, :] = high_deck[4:6]
    deck_ref[...] = wide[:, 0:80, :]
    w_columns, u_columns = wide[0].T, wide[1].T
    pieces = [low[0:16], own_ref[:, 0:128], own_ref[:, 128:256], high[0:16], tab_ref[...], w_columns[0:4], w_columns[124:128], u_columns[0:2], u_columns[126:128], jnp.zeros((4, 128), jnp.float32)]
    block = jnp.concatenate(pieces, axis=0)
    for t in range(4):
        out_ref[t, 0:EDGES, :] = block
        out_ref[t, EDGES:128, :] = edge_ref[0:40, :]
    out_ref[lax.rem(sect + 1, 4), EDGES:128, :] = edge_ref[40:80, :]


def wall_press(around_ref):
    lane = iota((8, 128), 1)
    low_half, y = lane < 64, lane & 63

    def get(t, c, z):
        part = around_ref[pl.ds(THIN + 16 * t + 3 * c + z, 4, stride=128), :]
        return jnp.concatenate([part, part], axis=0)

    def x_around(tiles):
        turned = [pltpu.roll(x, 64, 1) for x in tiles]
        after, before = turned[1:] + turned[-1:], turned[:1] + turned[:-1]
        ups = [jnp.where(low_half, a, b) for a, b in zip(turned, after)]
        downs = [jnp.where(low_half, b, a) for a, b in zip(turned, before)]
        return ups, downs

    def y_up(x):
        return jnp.where(y == 63, pltpu.roll(pltpu.roll(x, 7, 0), 63, 1), pltpu.roll(x, 127, 1))

    def y_down(x):
        return jnp.where(y == 0, pltpu.roll(pltpu.roll(x, 1, 0), 65, 1), pltpu.roll(x, 1, 1))

    def mirrored(state, prim):
        return [state[0], state[1], state[2], -state[3], state[4]], [prim[0], prim[1], -prim[2], prim[3], prim[4]]

    def advance(states, prims, layer, tiles):
        here, q = states[layer], prims[layer]
        xu = [x_around([here[t][c] for t in range(4)]) for c in range(5)]
        xq = {c: x_around([q[t][c] for t in range(4)]) for c in (0, 3, 4)}
        result = []
        for t in tiles:
            pack = [None] * 5
            up, down = [xu[c][0][t] for c in range(5)], [xu[c][1][t] for c in range(5)]
            upq, downq = list(pack), list(pack)
            for c in (0, 3, 4):
                upq[c], downq[c] = xq[c][0][t], xq[c][1][t]
            acc = add_direction(None, here[t], q[t], up, upq, down, downq, 0)
            up, down = [y_up(here[t][c]) for c in range(5)], [y_down(here[t][c]) for c in range(5)]
            upq, downq = list(pack), list(pack)
            for c in (1, 3, 4):
                upq[c], downq[c] = y_up(q[t][c]), y_down(q[t][c])
            acc = add_direction(acc, here[t], q[t], up, upq, down, downq, 1)
            down, downq = mirrored(here[t], q[t]) if layer == 0 else (states[layer - 1][t], prims[layer - 1][t])
            acc = add_direction(acc, here[t], q[t], states[layer + 1][t], prims[layer + 1][t], down, downq, 2)
            result.append([here[t][c] - KFL * acc[c] for c in range(5)])
        return result

    states, prims = [], []
    for z in range(3):
        both = [from_raw(*[get(t, c, z) for c in range(5)]) for t in range(4)]
        states.append([b[0] for b in both])
        prims.append([b[1] for b in both])
    after = [advance(states, prims, z, range(4)) for z in range(2)]
    after_prims = [[euler_prims(*after[z][t]) for t in range(4)] for z in range(2)]
    final = advance(after, after_prims, 0, (1, 2))
    return [euler_prims(*final[i])[3] for i in range(2)]


def by_seven(k):
    whole = (k * 9363) >> 16
    return whole, k - PER * whole


def gather_lanes(tables, cells):
    index = cells & 127
    low = jnp.take_along_axis(jnp.broadcast_to(tables[0], cells.shape), index, axis=1, mode="promise_in_bounds")
    high = jnp.take_along_axis(jnp.broadcast_to(tables[1], cells.shape), index, axis=1, mode="promise_in_bounds")
    return jnp.where(cells < 128, low, high) - AMBIENT


def facet_kernel(around_ref, cells_ref, tab_ref, pos_ref, out_hbm, press, out_ref, sems):
    sect = lax.axis_index("sect")
    left, right = side_rows()
    first, second = wall_press(around_ref)
    press[0:8, :] = first
    press[8:16, :] = second

    def tables(s):
        return press[pl.ds(s, 1), :], press[pl.ds(s + 8, 1), :]

    left_tab = around_ref[pl.ds(left + TABLE, 8), :]
    right_tab = around_ref[pl.ds(right + TABLE, 8), :]
    left_values = gather_lanes(tables(lax.rem(sect + 3, 4)), left_tab.astype(jnp.int32))
    right_values = gather_lanes(tables(lax.rem(sect + 1, 4)), right_tab.astype(jnp.int32))
    left_code = jnp.where(sect == 0, 0.0, left_tab[4:5])
    right_code = jnp.where(sect == 3, 0.0, right_tab[4:5])
    codes = jnp.concatenate([jnp.broadcast_to(x, (8, 128)) for x in (tab_ref[4:5, :], left_code, right_code)], axis=0)
    four = jnp.concatenate([left_values[2:4], right_values[0:2]], axis=0)
    eight = jnp.concatenate([four, four], axis=0)

    def weights(i):
        here = jnp.where((iota((24, 128), 0) & 7) == 2 + i, codes, 0.0)
        there = jnp.where((iota((8, 128), 0) >> 2) == i, eight, 0.0)
        return jnp.concatenate([here, jnp.zeros((48, 128), jnp.float32), there, jnp.zeros((48, 128), jnp.float32)], axis=0)

    o, p = iota((64, 256), 0), iota((64, 256), 1)
    base = pick(2 * o + (p >> 7) == (p & 127), jnp.concatenate([weights(0), weights(1)], axis=1), NT)
    owner, in_codes = iota((64, 128), 0), iota((64, 128), 1) < VALUES
    before = jnp.where(owner == 0, 0.0, pltpu.roll(base, 1, 0))
    after = jnp.where(owner == 63, 0.0, pltpu.roll(base, 63, 0))
    meta = base + jnp.where(in_codes, pltpu.roll(before, 126, 1), pltpu.roll(before, 120, 1))
    meta = meta + jnp.where(in_codes, pltpu.roll(after, 2, 1), pltpu.roll(after, 8, 1))
    parts = split3(gather_lanes(tables(sect), cells_ref[...]))
    copies = []
    size = 16 * PER
    for i in range(4):
        r = iota((size, 128), 0) + size * i
        whole, place = by_seven(r)
        chooser = (pos_ref[0:1, :].astype(jnp.int32) == 2 * whole + place - 2) & (place < 6)
        chooser = chooser.astype(jnp.float32).astype(jnp.bfloat16)
        total = None
        for part in parts:
            term = lax.dot_general(chooser, part, NN, preferred_element_type=jnp.float32)
            total = term if total is None else total + term
        out_ref[pl.ds(size * i, size), :] = total
        out_ref[pl.ds(size * i + 6, 16, stride=PER), :] = meta[16 * i : 16 * i + 16]
        copies.append(pltpu.make_async_copy(out_ref.at[pl.ds(size * i, size)], out_hbm.at[pl.ds(size * i, size)], sems.at[i]))
        copies[-1].start()
    for copy in copies:
        copy.wait()


def spread_sides(x):
    lanes = x.shape[1]
    return pltpu.roll(x, 1, 1) + pltpu.roll(x, lanes - 1, 1)


def early_kernel(around_ref, deck_ref, stiff_ref, tension_ref, anchor_ref, failed_ref, out_ref, turn):
    fluid, sect = lax.axis_index("fluid"), lax.axis_index("sect")
    left, right = side_rows()
    turn[...] = jnp.zeros((2, 128, 128), jnp.float32)
    turn[0, 0:4, :] = jnp.where(sect == 3, 0.0, around_ref[pl.ds(right + DECK, 4), :])
    turn[0, 124:128, :] = jnp.where(sect == 0, 0.0, around_ref[pl.ds(left + DECK + 4, 4), :])
    turn[1, 0:2, :] = jnp.where(sect == 3, 0.0, around_ref[pl.ds(right + DECK + 8, 2), :])
    turn[1, 126:128, :] = jnp.where(sect == 0, 0.0, around_ref[pl.ds(left + DECK + 10, 2), :])
    w = jnp.concatenate([deck_ref[0], turn[0].T[0:80]], axis=1)
    u = jnp.concatenate([deck_ref[1], turn[1].T[0:80]], axis=1)
    anchor = anchor_ref[...]
    count = anchor.shape[1]
    alive = iota((1, count), 1) != failed_ref[0]
    row = (anchor >> 9) - 64 * fluid + 8
    column = (anchor & 511) - 128 * sect
    lane = jnp.where((column >= -4) & (column < 132) & alive, column & 255, -1)
    rows = iota((80, count), 0) == row
    columns = iota((256, count), 0) == lane
    alpha = pick(rows, jnp.where(columns, stiff_ref[...], 0.0), NT)
    beta = pick(rows, jnp.where(columns, tension_ref[...], 0.0), NT)

    def laplace(x):
        return pltpu.roll(x, 1, 0) + pltpu.roll(x, 79, 0) + spread_sides(x) - 4.0 * x

    first = 2.0 * w - u + STEP_DECK * (beta - alpha * w - laplace(laplace(w)))
    r, c = iota((80, 256), 0) - 8, iota((80, 256), 1)
    c = jnp.where(c < 132, c, c - 256)
    g, h = r + 64 * fluid, c + 128 * sect
    inside = (g >= 0) & (g < 4096) & (h >= 0) & (h < 512) & (c >= -2) & (c < 130) & (r >= -2) & (r < 66)
    out_ref[0] = w
    out_ref[1] = jnp.where(inside, first, 0.0)
    out_ref[2] = alpha
    out_ref[3] = beta


def deck_kernel(got_ref, early_ref, deck_ref, ret_ref, spread, sides_ref, turn):
    count = 64 * PER
    meta = got_ref[pl.ds(6, 64, stride=PER), :]
    lane = iota((64, 128), 1)
    outer = (lane < 2) | (lane >= 126)
    for j in range(PER):
        spread[pl.ds(j, 64, stride=PER), :] = meta if j < 6 else jnp.zeros((64, 128), jnp.float32)
        turned = pltpu.roll(meta, (126 - VALUES - 4 * j) % 128, 1) if j < 6 else meta
        sides_ref[pl.ds(j, 64, stride=PER), :] = jnp.where(outer, turned, 0.0) if j < 6 else jnp.zeros((64, 128), jnp.float32)
    c = iota((count, 128), 1)
    own = jnp.where(((c & 7) == by_seven(iota((count, 128), 0))[1]) & (c < 24), spread[...], 0.0).astype(jnp.bfloat16)
    chooser = ((iota((16, 128), 1) >> 3) == iota((16, 128), 0)).astype(jnp.float32).astype(jnp.bfloat16)
    codes = lax.dot_general(chooser, own, NT, preferred_element_type=jnp.float32).astype(jnp.int32)
    place = by_seven(iota((1, count), 1))[1]
    offset = 64 * (place >> 1) - 64 + 8 - 128

    def rows_of(which):
        code = codes[which : which + 1]
        local = jnp.where(code > 0, code + offset, -1)
        return iota((80, count), 0) == local

    centre = pick(rows_of(0), got_ref[...])
    sides = pick(jnp.concatenate([rows_of(1), rows_of(2)], axis=0), sides_ref[...])
    edge = iota((80, 128), 1)
    sides = jnp.where(edge >= 126, sides[0:80], jnp.where(edge < 2, sides[80:160], 0.0))
    load = jnp.concatenate([centre, sides], axis=1)
    first = early_ref[1] + STEP_DECK * load
    turn[8:88, :] = first
    bend = turn[7:87, :] + turn[9:89, :] + spread_sides(first) - 4.0 * first
    turn[8:88, :] = bend
    bend = bend[8:72]
    around = spread_sides(bend)[:, 0:128]
    bend = turn[15:79, 0:128] + turn[17:81, 0:128] + around - 4.0 * bend[:, 0:128]
    own_rows = slice(8, 72)
    here = first[own_rows, 0:128]
    force = centre[own_rows] + early_ref[3, own_rows, 0:128] - early_ref[2, own_rows, 0:128] * here
    tile = 2.0 * here - early_ref[0, own_rows, 0:128] + STEP_DECK * (force - bend)
    deck_ref[...] = tile
    row = jnp.concatenate([meta[:, 2:3], meta[:, 3:4]], axis=0).astype(jnp.int32) - 128
    answer = pick(iota((128, 64), 1) == row, tile)
    for i in range(2):
        ret_ref[:, i, :] = answer[64 * i : 64 * i + 64]


def final_kernel(got_ref, place_ref, out_ref):
    out_ref[...] = pick(place_ref[...], got_ref[...])


def pack_kernel(raw_ref, around_ref, ext_ref, cor_ref):
    core = lax.axis_index("fluid") % 2
    left, right = side_rows()
    for ref, start in ((ext_ref, 2 * core), (cor_ref, 2 - 2 * core)):
        for c in range(5):
            for i in range(2):
                ref[c, i, 0:64, :] = raw_ref[c, start + i]
                ref[c, i, 64:66, :] = around_ref[pl.ds(right + EDGES + 8 * c + 2 * (start + i), 2), :]
                ref[c, i, 66:68, :] = around_ref[pl.ds(left + EDGES + 8 * c + 2 * (start + i), 2), :]
                ref[c, i, 68:72, :] = jnp.ones((4, 128), jnp.float32)


def bulk_kernel(raw_ref, ext_ref, cor_ref, around_ref, tile_ref, out_hbm, deck_hbm, ua, pa, ub, pb, result, sems):
    deck_copy = pltpu.make_async_copy(tile_ref, deck_hbm, sems.at[4])
    deck_copy.start()
    core = lax.axis_index("fluid") % 2
    left, right = side_rows()
    lane = lax.broadcasted_iota(jnp.int32, (8, 128), 1)
    first, last = lane == 0, lane == 127

    def put(planes, rows, raw):
        state, prim = from_raw(*raw)
        for c in range(5):
            ua[c, planes, rows, :] = state[c]
            pa[c, planes, rows, :] = prim[c]

    def own(i, _):
        for r in range(0, 64, 8):
            rows = pl.ds(r, 8)
            put(i + 2, pl.ds(r + YOFF, 8), [raw_ref[c, i, rows, :] for c in range(5)])
        put(i + 2, pl.ds(YOFF - 2, 2), [around_ref[pl.ds(left + EDGES + 8 * c + 2 * i, 2), :] for c in range(5)])
        put(i + 2, pl.ds(YOFF + 64, 2), [around_ref[pl.ds(right + EDGES + 8 * c + 2 * i, 2), :] for c in range(5)])
        return 0

    lax.fori_loop(0, 4, own, 0)

    def halo(i, _):
        for ref, base in ((ext_ref, 6 * core), (cor_ref, 6 - 6 * core)):
            for r in range(0, 64, 8):
                put(base + i, pl.ds(r + YOFF, 8), [ref[c, i, pl.ds(r, 8), :] for c in range(5)])
            put(base + i, pl.ds(YOFF + 64, 2), [ref[c, i, pl.ds(64, 2), :] for c in range(5)])
            put(base + i, pl.ds(YOFF - 2, 2), [ref[c, i, pl.ds(66, 2), :] for c in range(5)])
        return 0

    lax.fori_loop(0, 2, halo, 0)

    def update(u, q, i, r, n):
        def load(plane, row):
            rows = pl.ds(row, n)
            return [u[c, plane, rows, :] for c in range(5)], [q[c, plane, rows, :] for c in range(5)]

        here, prim = load(i, r)
        acc = None
        for d, (up, down) in enumerate((((i + 1, r), (i - 1, r)), ((i, r + 1), (i, r - 1)))):
            uu, uq = load(*up)
            du, dq = load(*down)
            acc = add_direction(acc, here, prim, uu, uq, du, dq, d)

        def shifted(x, sign, step, edge):
            return jnp.where(edge[:n], sign * x if sign < 0 else x, pltpu.roll(x, step, 1))

        signs = (1, 1, 1, -1, 1)
        qsigns = (None, None, -1, 1, 1)
        zu = [shifted(here[c], signs[c], 127, last) for c in range(5)]
        zd = [shifted(here[c], signs[c], 1, first) for c in range(5)]
        zuq = [None if qsigns[c] is None else shifted(prim[c], qsigns[c], 127, last) for c in range(5)]
        zdq = [None if qsigns[c] is None else shifted(prim[c], qsigns[c], 1, first) for c in range(5)]
        acc = add_direction(acc, here, prim, zu, zuq, zd, zdq, 2)
        return [here[c] - KFL * acc[c] for c in range(5)]

    def step_one(i, _):
        for r, n in [(YOFF - 8, 8)] + [(YOFF + k, 8) for k in range(0, 72, 8)]:
            if r == YOFF - 8:
                r, n = YOFF - 1, 1
            if r == YOFF + 64:
                n = 1
            new = update(ua, pa, i, r, n)
            prim = euler_prims(*new)
            for c in range(5):
                ub[c, i, pl.ds(r, n), :] = new[c]
                pb[c, i, pl.ds(r, n), :] = prim[c]
        return 0

    lax.fori_loop(1, 7, step_one, 0)

    def step_two(i, _):
        for r in range(0, 64, 8):
            new = update(ub, pb, i + 2, r + YOFF, 8)
            for c in range(5):
                result[c, i, pl.ds(r, 8), :] = new[c]
        return 0

    copies = []
    for i in range(4):
        step_two(i, 0)
        copies.append(pltpu.make_async_copy(result.at[:, i], out_hbm.at[:, i], sems.at[i]))
        copies[-1].start()
    for copy in copies:
        copy.wait()
    deck_copy.wait()


def bulk_euler(raw, ext, cor, around, tile):
    return local_call(
        bulk_kernel,
        [floats(5, 4, 64, 128), floats(64, 128)],
        "bulk_euler",
        (raw, ext, cor, around, tile),
        scratch=[pltpu.VMEM((5, 8, YROWS, 128), jnp.float32)] * 4 + [pltpu.VMEM((5, 4, 64, 128), jnp.float32), pltpu.SemaphoreType.DMA((5,))],
        flops=60_000_000,
        out_hbm=(0, 1),
    )


def body(
    density,
    velocity,
    pressure,
    deck_disp,
    deck_prev,
    stay_stiff,
    stay_tension,
    anchor_node,
    failed_stay,
    facet_cells,
    facet_owner,
    facet_row,
    facet_count,
):
    count = lax.axis_size("fluid")
    outward = [(i, (i + 1) % count if i % 2 else (i - 1) % count) for i in range(count)]
    inward = [(i, i ^ 1) for i in range(count)]
    raw, wu, ext, cor, own = local_call(
        prep_kernel,
        [floats(5, 4, 64, 128), floats(2, 64, 128), floats(24, 128), floats(24, 128), floats(16, 256)],
        "prep",
        (density, velocity, pressure, deck_disp, deck_prev),
        scratch=[pltpu.SemaphoreType.DMA((5,))],
        hbm=range(5),
    )
    ext = lax.ppermute(ext, "fluid", outward)
    cor = lax.ppermute(cor, "fluid", inward)
    tab, pos, place, cells, edge = local_call(
        table_kernel,
        [floats(8, 128), floats(8, 128), ((128, 128), jnp.bfloat16), ((128, 128), jnp.int32), floats(80, 128)],
        "tables",
        (facet_cells, facet_owner.reshape(1, -1), facet_row.reshape(1, -1), raw, facet_count),
        scratch=[pltpu.VMEM((16, 128), jnp.int32), pltpu.SemaphoreType.DMA((3,))],
        hbm=range(3),
        smem=(4,),
    )
    block, deck = local_call(
        middle_kernel,
        [floats(4, 128, 128), floats(2, 80, 128)],
        "middle",
        (ext, cor, own, wu, tab, edge),
        scratch=[pltpu.VMEM((2, 128, 128), jnp.float32)],
    )
    around = lax.all_to_all(block, "sect", split_axis=0, concat_axis=0, tiled=True).reshape(512, 128)
    (facets,) = local_call(
        facet_kernel,
        [floats(64 * PER, 128)],
        "facets",
        (around, cells, tab, pos),
        scratch=[pltpu.VMEM((16, 128), jnp.float32), pltpu.VMEM((64 * PER, 128), jnp.float32), pltpu.SemaphoreType.DMA((4,))],
        flops=4_000_000,
        out_hbm=(0,),
    )
    got = lax.all_to_all(facets.reshape(64, 1, PER * 128), "fluid", split_axis=0, concat_axis=0, tiled=True).reshape(64 * PER, 128)
    (early,) = local_call(
        early_kernel,
        [floats(4, 80, 256)],
        "early_deck",
        (around, deck, stay_stiff.reshape(1, -1), stay_tension.reshape(1, -1), anchor_node.reshape(1, -1), failed_stay),
        scratch=[pltpu.VMEM((2, 128, 128), jnp.float32)],
        smem=(5,),
    )
    ext_planes, cor_planes = local_call(pack_kernel, [floats(5, 2, 72, 128), floats(5, 2, 72, 128)], "pack", (raw, around))
    ext_planes = lax.ppermute(ext_planes, "fluid", outward)
    cor_planes = lax.ppermute(cor_planes, "fluid", inward)
    tile, back = local_call(
        deck_kernel,
        [floats(64, 128), floats(64, 2, 128)],
        "deck",
        (got, early),
        scratch=[pltpu.VMEM((64 * PER, 128), jnp.float32)] * 2 + [pltpu.VMEM((96, 256), jnp.float32)],
        flops=4_000_000,
    )
    back = lax.all_to_all(back, "fluid", split_axis=0, concat_axis=0, tiled=True)
    fields, deck_next = bulk_euler(raw, ext_planes, cor_planes, around, tile)
    (facet_disp,) = local_call(final_kernel, [floats(128, 128)], "final", (back.reshape(128, 128), place), free=True)
    return (fields, deck_next, facet_disp)


def solution(mesh):
    return jax.shard_map(
        body,
        mesh=mesh,
        in_specs=(
            P("fluid", "sect", None),
            P(None, "fluid", "sect", None),
            P("fluid", "sect", None),
            P("fluid", "sect"),
            P("fluid", "sect"),
            P(),
            P(),
            P(),
            P(),
            P(("fluid", "sect"), None),
            P(("fluid", "sect"), None),
            P(("fluid", "sect")),
            P(("fluid", "sect")),
        ),
        out_specs=(P(None, "fluid", "sect", None), P("fluid", "sect"), P(("fluid", "sect"), None)),
        check_vma=False,
    )
```

```python
import jax
import jax.numpy as jnp
from jax import lax
from jax.experimental import pallas as pl
from jax.experimental.pallas import tpu as pltpu
from jax.sharding import PartitionSpec as P

STEP_FLUID = 0.045
STEP_DECK = 0.06
GAMMA_LESS = 0.4
AMBIENT = 1.0

TABLE = 64
DECK = 72
EDGES = 80
BLOCK = 120
PER = 7
VALUES = 64
NT = (((1,), (1,)), ((), ()))
NN = (((1,), (0,)), ((), ()))


def local_call(kernel, shapes, name, args, scratch=(), flops=1_000_000, smem=(), hbm=(), out_hbm=(), free=False):
    outs = [jax.ShapeDtypeStruct(*s) if free else pltpu.HBM(*s) if i in out_hbm else pltpu.VMEM(*s) for i, s in enumerate(shapes)]
    spaces = [pltpu.SMEM if i in smem else pltpu.HBM if i in hbm else pltpu.VMEM for i in range(len(args))]
    args = [pltpu.with_memory_space_constraint(a, pltpu.HBM) if i in hbm else a for i, a in enumerate(args)]
    return pl.pallas_call(
        kernel,
        out_shape=outs,
        in_specs=[pl.BlockSpec(memory_space=s) for s in spaces],
        out_specs=[pl.BlockSpec(memory_space=pltpu.HBM if i in out_hbm else pltpu.VMEM) for i in range(len(outs))],
        scratch_shapes=list(scratch),
        compiler_params=pltpu.CompilerParams(vmem_limit_bytes=32 * 1024 * 1024),
        cost_estimate=pl.CostEstimate(flops=flops, bytes_accessed=1_000_000, transcendentals=0),
        name=name,
    )(*args)


def floats(*shape):
    return shape, jnp.float32


def iota(shape, axis):
    return lax.broadcasted_iota(jnp.int32, shape, axis)


def split3(x):
    high = x.astype(jnp.bfloat16)
    rest = x - high.astype(jnp.float32)
    middle = rest.astype(jnp.bfloat16)
    low = (rest - middle.astype(jnp.float32)).astype(jnp.bfloat16)
    return high, middle, low


def pick(onehot, table, dims=NN):
    onehot = onehot.astype(jnp.float32).astype(jnp.bfloat16)
    total = None
    for part in split3(table):
        term = lax.dot_general(onehot, part, dims, preferred_element_type=jnp.float32)
        total = term if total is None else total + term
    return total


YOFF = 8
YROWS = 80
KFL = 0.5 * STEP_FLUID


def euler_prims(rho, m1, m2, m3, en):
    inv = 1.0 / rho
    v1, v2, v3 = m1 * inv, m2 * inv, m3 * inv
    p = GAMMA_LESS * (en - 0.5 * (m1 * v1 + m2 * v2 + m3 * v3))
    return v1, v2, v3, p, jnp.sqrt(1.4 * p * inv)


def from_raw(rho, v1, v2, v3, p):
    en = p * (1.0 / GAMMA_LESS) + 0.5 * rho * (v1 * v1 + v2 * v2 + v3 * v3)
    return (rho, rho * v1, rho * v2, rho * v3, en), (v1, v2, v3, p, jnp.sqrt(1.4 * p / rho))


def flux(state, prim, d):
    rho, m1, m2, m3, en = state
    v, p = prim[d], prim[3]
    out = [state[1 + d], m1 * v, m2 * v, m3 * v, (en + p) * v]
    out[1 + d] = out[1 + d] + p
    return out


def add_direction(acc, here, prim, up, uprim, down, dprim, d):
    fu, fd = flux(up, uprim, d), flux(down, dprim, d)
    s0 = jnp.abs(prim[d]) + prim[4]
    lu = jnp.maximum(s0, jnp.abs(uprim[d]) + uprim[4])
    ld = jnp.maximum(s0, jnp.abs(dprim[d]) + dprim[4])
    out = []
    for c in range(5):
        term = (fu[c] - fd[c]) - lu * (up[c] - here[c]) + ld * (here[c] - down[c])
        out.append(term if acc is None else acc[c] + term)
    return out


def prep_kernel(rho_hbm, vel_hbm, pre_hbm, w_hbm, u_hbm, cells_hbm, owner_hbm, row_hbm, raw_ref, wu_ref, ext_ref, cor_ref, own_ref, cells_ref, slots_ref, sems):
    core = lax.axis_index("fluid") % 2
    pairs = [
        (rho_hbm, raw_ref.at[0]),
        (vel_hbm, raw_ref.at[pl.ds(1, 3)]),
        (pre_hbm, raw_ref.at[4]),
        (w_hbm, wu_ref.at[0]),
        (u_hbm, wu_ref.at[1]),
        (cells_hbm, cells_ref),
        (owner_hbm, slots_ref.at[pl.ds(0, 1)]),
        (row_hbm, slots_ref.at[pl.ds(8, 1)]),
    ]
    copies = [pltpu.make_async_copy(a, b, sems.at[i]) for i, (a, b) in enumerate(pairs)]
    for copy in copies:
        copy.start()
    chooser = iota((16, 128), 0) == iota((16, 128), 1)
    own_ref[15:16, :] = jnp.zeros((1, 256), jnp.float32)
    ext_ref[22:24, :] = jnp.zeros((2, 128), jnp.float32)
    cor_ref[22:24, :] = jnp.zeros((2, 128), jnp.float32)
    for copy in copies[:5]:
        copy.wait()
    for c in range(5):
        own_ref[3 * c : 3 * c + 3, :] = pick(chooser, raw_ref[c].reshape(256, 128), NT)[0:3]
    first, last = own_ref[:, 0:128], own_ref[:, 128:256]
    even = core == 0
    ext_ref[0:16, :] = jnp.where(even, first, last)
    cor_ref[0:16, :] = jnp.where(even, last, first)
    wf, wl, uf, ul = wu_ref[0, 0:4, :], wu_ref[0, 60:64, :], wu_ref[1, 0:2, :], wu_ref[1, 62:64, :]
    ext_ref[16:20, :] = jnp.where(even, wf, wl)
    cor_ref[16:20, :] = jnp.where(even, wl, wf)
    ext_ref[20:22, :] = jnp.where(even, uf, ul)
    cor_ref[20:22, :] = jnp.where(even, ul, uf)
    for copy in copies[5:]:
        copy.wait()


def table_kernel(cells_ref, slots_ref, raw_ref, count_ref, tab_ref, pos_ref, place_ref, edge_ref):
    for c in range(5):
        for side, y in ((0, 0), (1, 62)):
            for i in range(4):
                edge_ref[side, pl.ds(8 * c + 2 * i, 2), :] = raw_ref[c, i, pl.ds(y, 2), :]
    owner_row = jnp.broadcast_to(slots_ref[0:1, :].astype(jnp.float32), (128, 128))
    owner = owner_row.T
    same = owner == owner_row
    down, along = iota((128, 128), 0), iota((128, 128), 1)
    within = jnp.sum(jnp.where(same & (along < down), 1.0, 0.0), axis=1, keepdims=True)
    within_row = jnp.sum(jnp.where(same & (down < along), 1.0, 0.0), axis=0, keepdims=True)
    position = (2.0 * owner[:, 0:1] + within).astype(jnp.int32)
    pos_ref[...] = jnp.broadcast_to(2.0 * owner_row[0:1, :] + within_row, (8, 128))
    place = jnp.where(position == along, 1.0, 0.0).astype(jnp.bfloat16)
    place_ref[...] = place
    r, c = iota((16, 128), 0), iota((16, 128), 1)
    columns = jnp.where(((r < 2) & (c == r)) | ((r >= 2) & (r < 4) & (c == r + 124)), 1.0, 0.0).astype(jnp.bfloat16)
    cells = cells_ref[...].astype(jnp.float32).astype(jnp.bfloat16)
    picked = lax.dot_general(columns, cells, NT, preferred_element_type=jnp.float32)
    live = iota((1, 128), 1) < count_ref[...]
    code = jnp.where(live, slots_ref[8:9, :] + 128, 0).astype(jnp.float32)
    stacked = jnp.where(r == 4, jnp.broadcast_to(code, (16, 128)), picked).astype(jnp.bfloat16)
    tab_ref[...] = lax.dot_general(stacked, place, NN, preferred_element_type=jnp.float32)[0:8]


def middle_kernel(ext_ref, cor_ref, own_ref, wu_ref, tab_ref, edge_ref, up_ref, down_ref, far_ref, deck_ref, wide):
    fluid = lax.axis_index("fluid")
    even = fluid % 2 == 0
    ext, cor = ext_ref[...], cor_ref[...]
    low, high = jnp.where(even, ext, cor), jnp.where(even, cor, ext)
    low_deck = jnp.where(fluid == 0, 0.0, low[16:24])
    high_deck = jnp.where(fluid == 63, 0.0, high[16:24])
    wide[...] = jnp.zeros((2, 128, 128), jnp.float32)
    wide[0, 4:8, :] = low_deck[0:4]
    wide[0, 8:72, :] = wu_ref[0]
    wide[0, 72:76, :] = high_deck[0:4]
    wide[1, 6:8, :] = low_deck[4:6]
    wide[1, 8:72, :] = wu_ref[1]
    wide[1, 72:74, :] = high_deck[4:6]
    deck_ref[...] = wide[:, 0:80, :]
    w_columns, u_columns = wide[0].T, wide[1].T
    tiles = [low[0:16], own_ref[:, 0:128], own_ref[:, 128:256], high[0:16]]
    pad = jnp.zeros((2, 128), jnp.float32)
    for ref, side, w_part, u_part in ((up_ref, 1, w_columns[124:128], u_columns[126:128]), (down_ref, 0, w_columns[0:4], u_columns[0:2])):
        ref[0:80, :] = jnp.concatenate(tiles + [tab_ref[...], w_part, u_part, pad], axis=0)
        ref[EDGES:BLOCK, :] = edge_ref[side]
    y = iota((16, 128), 1) & 63
    rim = (y < 2) | (y >= 62)
    far_ref[...] = sum(pltpu.roll(jnp.where(rim, x, 0.0), 4 * i, 1) if i else jnp.where(rim, x, 0.0) for i, x in enumerate(tiles))


def wall_press(thin):
    lane = iota((8, 128), 1)
    low_half, y = lane < 64, lane & 63

    def get(t, c, z):
        part = thin[pl.ds(16 * t + 3 * c + z, 4, stride=64), :]
        return jnp.concatenate([part, part], axis=0)

    def x_around(tiles):
        turned = [pltpu.roll(x, 64, 1) for x in tiles]
        after, before = turned[1:] + turned[-1:], turned[:1] + turned[:-1]
        ups = [jnp.where(low_half, a, b) for a, b in zip(turned, after)]
        downs = [jnp.where(low_half, b, a) for a, b in zip(turned, before)]
        return ups, downs

    def y_up(x):
        return jnp.where(y == 63, pltpu.roll(pltpu.roll(x, 7, 0), 63, 1), pltpu.roll(x, 127, 1))

    def y_down(x):
        return jnp.where(y == 0, pltpu.roll(pltpu.roll(x, 1, 0), 65, 1), pltpu.roll(x, 1, 1))

    def mirrored(state, prim):
        return [state[0], state[1], state[2], -state[3], state[4]], [prim[0], prim[1], -prim[2], prim[3], prim[4]]

    def advance(states, prims, layer, tiles):
        here, q = states[layer], prims[layer]
        xu = [x_around([here[t][c] for t in range(4)]) for c in range(5)]
        xq = {c: x_around([q[t][c] for t in range(4)]) for c in (0, 3, 4)}
        result = []
        for t in tiles:
            pack = [None] * 5
            up, down = [xu[c][0][t] for c in range(5)], [xu[c][1][t] for c in range(5)]
            upq, downq = list(pack), list(pack)
            for c in (0, 3, 4):
                upq[c], downq[c] = xq[c][0][t], xq[c][1][t]
            acc = add_direction(None, here[t], q[t], up, upq, down, downq, 0)
            up, down = [y_up(here[t][c]) for c in range(5)], [y_down(here[t][c]) for c in range(5)]
            upq, downq = list(pack), list(pack)
            for c in (1, 3, 4):
                upq[c], downq[c] = y_up(q[t][c]), y_down(q[t][c])
            acc = add_direction(acc, here[t], q[t], up, upq, down, downq, 1)
            down, downq = mirrored(here[t], q[t]) if layer == 0 else (states[layer - 1][t], prims[layer - 1][t])
            acc = add_direction(acc, here[t], q[t], states[layer + 1][t], prims[layer + 1][t], down, downq, 2)
            result.append([here[t][c] - KFL * acc[c] for c in range(5)])
        return result

    states, prims = [], []
    for z in range(3):
        both = [from_raw(*[get(t, c, z) for c in range(5)]) for t in range(4)]
        states.append([b[0] for b in both])
        prims.append([b[1] for b in both])
    after = [advance(states, prims, z, range(4)) for z in range(2)]
    after_prims = [[euler_prims(*after[z][t]) for t in range(4)] for z in range(2)]
    final = advance(after, after_prims, 0, (1, 2))
    return [euler_prims(*final[i])[3] for i in range(2)]


def by_seven(k):
    whole = (k * 9363) >> 16
    return whole, k - PER * whole


def gather_lanes(tables, cells):
    index = cells & 127
    low = jnp.take_along_axis(jnp.broadcast_to(tables[0], cells.shape), index, axis=1, mode="promise_in_bounds")
    high = jnp.take_along_axis(jnp.broadcast_to(tables[1], cells.shape), index, axis=1, mode="promise_in_bounds")
    return jnp.where(cells < 128, low, high) - AMBIENT


def facet_kernel(up_ref, left_ref, right_ref, far_ref, cells_ref, tab_ref, pos_ref, out_hbm, thin, press, out_ref, sems):
    sect = lax.axis_index("sect")
    for i, ref in ((0, up_ref), (1, right_ref), (3, left_ref)):
        thin[64 * i : 64 * i + 64, :] = ref[0:64, :]
    far = far_ref[...]
    for i in range(4):
        thin[128 + 16 * i : 144 + 16 * i, :] = pltpu.roll(far, 128 - 4 * i, 1) if i else far
    first, second = wall_press(thin)
    press[0:8, :] = first
    press[8:16, :] = second

    def tables(s):
        return press[s : s + 1, :], press[s + 8 : s + 9, :]

    left_tab, right_tab = left_ref[TABLE : TABLE + 8, :], right_ref[TABLE : TABLE + 8, :]
    left_values = gather_lanes(tables(3), left_tab.astype(jnp.int32))
    right_values = gather_lanes(tables(1), right_tab.astype(jnp.int32))
    left_code = jnp.where(sect == 0, 0.0, left_tab[4:5])
    right_code = jnp.where(sect == 3, 0.0, right_tab[4:5])
    codes = jnp.concatenate([jnp.broadcast_to(x, (8, 128)) for x in (tab_ref[4:5, :], left_code, right_code)], axis=0)
    four = jnp.concatenate([left_values[2:4], right_values[0:2]], axis=0)
    eight = jnp.concatenate([four, four], axis=0)

    def weights(i):
        here = jnp.where((iota((24, 128), 0) & 7) == 2 + i, codes, 0.0)
        there = jnp.where((iota((8, 128), 0) >> 2) == i, eight, 0.0)
        return jnp.concatenate([here, jnp.zeros((48, 128), jnp.float32), there, jnp.zeros((48, 128), jnp.float32)], axis=0)

    o, p = iota((64, 256), 0), iota((64, 256), 1)
    base = pick(2 * o + (p >> 7) == (p & 127), jnp.concatenate([weights(0), weights(1)], axis=1), NT)
    owner, in_codes = iota((64, 128), 0), iota((64, 128), 1) < VALUES
    before = jnp.where(owner == 0, 0.0, pltpu.roll(base, 1, 0))
    after = jnp.where(owner == 63, 0.0, pltpu.roll(base, 63, 0))
    meta = base + jnp.where(in_codes, pltpu.roll(before, 126, 1), pltpu.roll(before, 120, 1))
    meta = meta + jnp.where(in_codes, pltpu.roll(after, 2, 1), pltpu.roll(after, 8, 1))
    parts = split3(gather_lanes(tables(0), cells_ref[...]))
    copies = []
    size = 16 * PER
    for i in range(4):
        r = iota((size, 128), 0) + size * i
        whole, place = by_seven(r)
        chooser = (pos_ref[0:1, :].astype(jnp.int32) == 2 * whole + place - 2) & (place < 6)
        chooser = chooser.astype(jnp.float32).astype(jnp.bfloat16)
        total = None
        for part in parts:
            term = lax.dot_general(chooser, part, NN, preferred_element_type=jnp.float32)
            total = term if total is None else total + term
        out_ref[pl.ds(size * i, size), :] = total
        out_ref[pl.ds(size * i + 6, 16, stride=PER), :] = meta[16 * i : 16 * i + 16]
        copies.append(pltpu.make_async_copy(out_ref.at[pl.ds(size * i, size)], out_hbm.at[pl.ds(size * i, size)], sems.at[i]))
        copies[-1].start()
    for copy in copies:
        copy.wait()


def spread_sides(x):
    lanes = x.shape[1]
    return pltpu.roll(x, 1, 1) + pltpu.roll(x, lanes - 1, 1)


def early_kernel(left_ref, right_ref, deck_ref, stiff_ref, tension_ref, anchor_ref, failed_ref, out_ref, turn):
    fluid, sect = lax.axis_index("fluid"), lax.axis_index("sect")
    turn[...] = jnp.zeros((2, 128, 128), jnp.float32)
    from_left = jnp.where(sect == 0, 0.0, left_ref[DECK : DECK + 8, :])
    from_right = jnp.where(sect == 3, 0.0, right_ref[DECK : DECK + 8, :])
    turn[0, 0:4, :] = from_right[0:4]
    turn[0, 124:128, :] = from_left[0:4]
    turn[1, 0:2, :] = from_right[4:6]
    turn[1, 126:128, :] = from_left[4:6]
    w = jnp.concatenate([deck_ref[0], turn[0].T[0:80]], axis=1)
    u = jnp.concatenate([deck_ref[1], turn[1].T[0:80]], axis=1)
    anchor = anchor_ref[...]
    count = anchor.shape[1]
    alive = iota((1, count), 1) != failed_ref[0]
    row = (anchor >> 9) - 64 * fluid + 8
    column = (anchor & 511) - 128 * sect
    lane = jnp.where((column >= -4) & (column < 132) & alive, column & 255, -1)
    rows = iota((80, count), 0) == row
    columns = iota((256, count), 0) == lane
    alpha = pick(rows, jnp.where(columns, stiff_ref[...], 0.0), NT)
    beta = pick(rows, jnp.where(columns, tension_ref[...], 0.0), NT)

    def laplace(x):
        return pltpu.roll(x, 1, 0) + pltpu.roll(x, 79, 0) + spread_sides(x) - 4.0 * x

    first = 2.0 * w - u + STEP_DECK * (beta - alpha * w - laplace(laplace(w)))
    r, c = iota((80, 256), 0) - 8, iota((80, 256), 1)
    c = jnp.where(c < 132, c, c - 256)
    g, h = r + 64 * fluid, c + 128 * sect
    inside = (g >= 0) & (g < 4096) & (h >= 0) & (h < 512) & (c >= -2) & (c < 130) & (r >= -2) & (r < 66)
    out_ref[0] = w
    out_ref[1] = jnp.where(inside, first, 0.0)
    out_ref[2] = alpha
    out_ref[3] = beta


def deck_kernel(got_ref, early_ref, deck_ref, ret_ref, spread, sides_ref, turn):
    count = 64 * PER
    meta = got_ref[pl.ds(6, 64, stride=PER), :]
    lane = iota((64, 128), 1)
    outer = (lane < 2) | (lane >= 126)
    for j in range(PER):
        spread[pl.ds(j, 64, stride=PER), :] = meta if j < 6 else jnp.zeros((64, 128), jnp.float32)
        turned = pltpu.roll(meta, (126 - VALUES - 4 * j) % 128, 1) if j < 6 else meta
        sides_ref[pl.ds(j, 64, stride=PER), :] = jnp.where(outer, turned, 0.0) if j < 6 else jnp.zeros((64, 128), jnp.float32)
    c = iota((count, 128), 1)
    own = jnp.where(((c & 7) == by_seven(iota((count, 128), 0))[1]) & (c < 24), spread[...], 0.0).astype(jnp.bfloat16)
    chooser = ((iota((16, 128), 1) >> 3) == iota((16, 128), 0)).astype(jnp.float32).astype(jnp.bfloat16)
    codes = lax.dot_general(chooser, own, NT, preferred_element_type=jnp.float32).astype(jnp.int32)
    place = by_seven(iota((1, count), 1))[1]
    offset = 64 * (place >> 1) - 64 + 8 - 128

    def rows_of(which):
        code = codes[which : which + 1]
        local = jnp.where(code > 0, code + offset, -1)
        return iota((80, count), 0) == local

    centre = pick(rows_of(0), got_ref[...])
    sides = pick(jnp.concatenate([rows_of(1), rows_of(2)], axis=0), sides_ref[...])
    edge = iota((80, 128), 1)
    sides = jnp.where(edge >= 126, sides[0:80], jnp.where(edge < 2, sides[80:160], 0.0))
    load = jnp.concatenate([centre, sides], axis=1)
    first = early_ref[1] + STEP_DECK * load
    turn[8:88, :] = first

    def at(step):
        return turn[16 + step : 80 + step, :]

    here = at(0)
    near, two = at(1) + at(-1), at(2) + at(-2)
    cross = 2.0 * near - 8.0 * here
    bend = 20.0 * here - 8.0 * near + two
    for x, step in ((cross, 1), (here, 2)):
        bend = bend + pltpu.roll(x, step, 1) + pltpu.roll(x, 256 - step, 1)
    bend = bend[:, 0:128]
    own_rows = slice(8, 72)
    here = here[:, 0:128]
    force = centre[own_rows] + early_ref[3, own_rows, 0:128] - early_ref[2, own_rows, 0:128] * here
    tile = 2.0 * here - early_ref[0, own_rows, 0:128] + STEP_DECK * (force - bend)
    deck_ref[...] = tile
    row = jnp.concatenate([meta[:, 2:3], meta[:, 3:4]], axis=0).astype(jnp.int32) - 128
    answer = pick(iota((128, 64), 1) == row, tile)
    for i in range(2):
        ret_ref[:, i, :] = answer[64 * i : 64 * i + 64]


def final_kernel(got_ref, place_ref, out_ref):
    out_ref[...] = pick(place_ref[...], got_ref[...])


def pack_kernel(raw_ref, left_ref, right_ref, ext_ref, cor_ref):
    core = lax.axis_index("fluid") % 2
    for ref, start in ((ext_ref, 2 * core), (cor_ref, 2 - 2 * core)):
        for c in range(5):
            for i in range(2):
                ref[c, i, 0:64, :] = raw_ref[c, start + i]
                ref[c, i, 64:66, :] = right_ref[pl.ds(EDGES + 8 * c + 2 * (start + i), 2), :]
                ref[c, i, 66:68, :] = left_ref[pl.ds(EDGES + 8 * c + 2 * (start + i), 2), :]
                ref[c, i, 68:72, :] = jnp.ones((4, 128), jnp.float32)


def bulk_kernel(raw_ref, ext_ref, cor_ref, left_ref, right_ref, tile_ref, out_hbm, deck_hbm, ua, pa, ub, pb, result, sems):
    deck_copy = pltpu.make_async_copy(tile_ref, deck_hbm, sems.at[4])
    deck_copy.start()
    core = lax.axis_index("fluid") % 2
    lane = lax.broadcasted_iota(jnp.int32, (8, 128), 1)
    first, last = lane == 0, lane == 127

    def put(planes, rows, raw):
        state, prim = from_raw(*raw)
        for c in range(5):
            ua[c, planes, rows, :] = state[c]
            pa[c, planes, rows, :] = prim[c]

    def own(i, _):
        for r in range(0, 64, 8):
            rows = pl.ds(r, 8)
            put(i + 2, pl.ds(r + YOFF, 8), [raw_ref[c, i, rows, :] for c in range(5)])
        put(i + 2, pl.ds(YOFF - 2, 2), [left_ref[pl.ds(EDGES + 8 * c + 2 * i, 2), :] for c in range(5)])
        put(i + 2, pl.ds(YOFF + 64, 2), [right_ref[pl.ds(EDGES + 8 * c + 2 * i, 2), :] for c in range(5)])
        return 0

    lax.fori_loop(0, 4, own, 0)

    def halo(i, _):
        for ref, base in ((ext_ref, 6 * core), (cor_ref, 6 - 6 * core)):
            for r in range(0, 64, 8):
                put(base + i, pl.ds(r + YOFF, 8), [ref[c, i, pl.ds(r, 8), :] for c in range(5)])
            put(base + i, pl.ds(YOFF + 64, 2), [ref[c, i, pl.ds(64, 2), :] for c in range(5)])
            put(base + i, pl.ds(YOFF - 2, 2), [ref[c, i, pl.ds(66, 2), :] for c in range(5)])
        return 0

    lax.fori_loop(0, 2, halo, 0)

    def update(u, q, i, r, n):
        def load(plane, row):
            rows = pl.ds(row, n)
            return [u[c, plane, rows, :] for c in range(5)], [q[c, plane, rows, :] for c in range(5)]

        here, prim = load(i, r)
        acc = None
        for d, (up, down) in enumerate((((i + 1, r), (i - 1, r)), ((i, r + 1), (i, r - 1)))):
            uu, uq = load(*up)
            du, dq = load(*down)
            acc = add_direction(acc, here, prim, uu, uq, du, dq, d)

        def shifted(x, sign, step, edge):
            return jnp.where(edge[:n], sign * x if sign < 0 else x, pltpu.roll(x, step, 1))

        signs = (1, 1, 1, -1, 1)
        qsigns = (None, None, -1, 1, 1)
        zu = [shifted(here[c], signs[c], 127, last) for c in range(5)]
        zd = [shifted(here[c], signs[c], 1, first) for c in range(5)]
        zuq = [None if qsigns[c] is None else shifted(prim[c], qsigns[c], 127, last) for c in range(5)]
        zdq = [None if qsigns[c] is None else shifted(prim[c], qsigns[c], 1, first) for c in range(5)]
        acc = add_direction(acc, here, prim, zu, zuq, zd, zdq, 2)
        return [here[c] - KFL * acc[c] for c in range(5)]

    def step_one(i, _):
        for r, n in [(YOFF - 8, 8)] + [(YOFF + k, 8) for k in range(0, 72, 8)]:
            if r == YOFF - 8:
                r, n = YOFF - 1, 1
            if r == YOFF + 64:
                n = 1
            new = update(ua, pa, i, r, n)
            prim = euler_prims(*new)
            for c in range(5):
                ub[c, i, pl.ds(r, n), :] = new[c]
                pb[c, i, pl.ds(r, n), :] = prim[c]
        return 0

    lax.fori_loop(1, 7, step_one, 0)

    def step_two(i, _):
        for r in range(0, 64, 8):
            new = update(ub, pb, i + 2, r + YOFF, 8)
            for c in range(5):
                result[c, i, pl.ds(r, 8), :] = new[c]
        return 0

    copies = []
    for i in range(4):
        step_two(i, 0)
        copies.append(pltpu.make_async_copy(result.at[:, i], out_hbm.at[:, i], sems.at[i]))
        copies[-1].start()
    for copy in copies:
        copy.wait()
    deck_copy.wait()


def bulk_euler(raw, ext, cor, left, right, tile):
    return local_call(
        bulk_kernel,
        [floats(5, 4, 64, 128), floats(64, 128)],
        "bulk_euler",
        (raw, ext, cor, left, right, tile),
        scratch=[pltpu.VMEM((5, 8, YROWS, 128), jnp.float32)] * 4 + [pltpu.VMEM((5, 4, 64, 128), jnp.float32), pltpu.SemaphoreType.DMA((5,))],
        flops=60_000_000,
        out_hbm=(0, 1),
    )


def body(
    density,
    velocity,
    pressure,
    deck_disp,
    deck_prev,
    stay_stiff,
    stay_tension,
    anchor_node,
    failed_stay,
    facet_cells,
    facet_owner,
    facet_row,
    facet_count,
):
    count = lax.axis_size("fluid")
    outward = [(i, (i + 1) % count if i % 2 else (i - 1) % count) for i in range(count)]
    inward = [(i, i ^ 1) for i in range(count)]
    raw, wu, ext, cor, own, cells, slots = local_call(
        prep_kernel,
        [floats(5, 4, 64, 128), floats(2, 64, 128), floats(24, 128), floats(24, 128), floats(16, 256), ((128, 128), jnp.int32), ((16, 128), jnp.int32)],
        "prep",
        (density, velocity, pressure, deck_disp, deck_prev, facet_cells, facet_owner.reshape(1, -1), facet_row.reshape(1, -1)),
        scratch=[pltpu.SemaphoreType.DMA((8,))],
        hbm=range(8),
    )
    ext = lax.ppermute(ext, "fluid", outward)
    cor = lax.ppermute(cor, "fluid", inward)
    tab, pos, place, edge = local_call(
        table_kernel, [floats(8, 128), floats(8, 128), ((128, 128), jnp.bfloat16), floats(2, 40, 128)], "tables", (cells, slots, raw, facet_count.reshape(1, 1))
    )
    up, down, far, deck = local_call(
        middle_kernel,
        [floats(BLOCK, 128), floats(BLOCK, 128), floats(16, 128), floats(2, 80, 128)],
        "middle",
        (ext, cor, own, wu, tab, edge),
        scratch=[pltpu.VMEM((2, 128, 128), jnp.float32)],
    )
    around = lax.axis_size("sect")
    forward = [(i, (i + 1) % around) for i in range(around)]
    backward = [(i, (i - 1) % around) for i in range(around)]
    far = lax.ppermute(far, "sect", [(i, (i + 2) % around) for i in range(around)])
    left = lax.ppermute(up, "sect", forward)
    right = lax.ppermute(down, "sect", backward)
    (facets,) = local_call(
        facet_kernel,
        [floats(64 * PER, 128)],
        "facets",
        (up, left, right, far, cells, tab, pos),
        scratch=[pltpu.VMEM((256, 128), jnp.float32), pltpu.VMEM((16, 128), jnp.float32), pltpu.VMEM((64 * PER, 128), jnp.float32), pltpu.SemaphoreType.DMA((4,))],
        flops=4_000_000,
        out_hbm=(0,),
    )
    got = lax.all_to_all(facets.reshape(64, 1, PER * 128), "fluid", split_axis=0, concat_axis=0, tiled=True).reshape(64 * PER, 128)
    (early,) = local_call(
        early_kernel,
        [floats(4, 80, 256)],
        "early_deck",
        (left, right, deck, stay_stiff.reshape(1, -1), stay_tension.reshape(1, -1), anchor_node.reshape(1, -1), failed_stay),
        scratch=[pltpu.VMEM((2, 128, 128), jnp.float32)],
        smem=(6,),
    )
    ext_planes, cor_planes = local_call(pack_kernel, [floats(5, 2, 72, 128), floats(5, 2, 72, 128)], "pack", (raw, left, right))
    ext_planes = lax.ppermute(ext_planes, "fluid", outward)
    cor_planes = lax.ppermute(cor_planes, "fluid", inward)
    tile, back = local_call(
        deck_kernel,
        [floats(64, 128), floats(64, 2, 128)],
        "deck",
        (got, early),
        scratch=[pltpu.VMEM((64 * PER, 128), jnp.float32)] * 2 + [pltpu.VMEM((96, 256), jnp.float32)],
        flops=4_000_000,
    )
    back = lax.all_to_all(back, "fluid", split_axis=0, concat_axis=0, tiled=True)
    fields, deck_next = bulk_euler(raw, ext_planes, cor_planes, left, right, tile)
    (facet_disp,) = local_call(final_kernel, [floats(128, 128)], "final", (back.reshape(128, 128), place), free=True)
    return (fields, deck_next, facet_disp)


def solution(mesh):
    return jax.shard_map(
        body,
        mesh=mesh,
        in_specs=(
            P("fluid", "sect", None),
            P(None, "fluid", "sect", None),
            P("fluid", "sect", None),
            P("fluid", "sect"),
            P("fluid", "sect"),
            P(),
            P(),
            P(),
            P(),
            P(("fluid", "sect"), None),
            P(("fluid", "sect"), None),
            P(("fluid", "sect")),
            P(("fluid", "sect")),
        ),
        out_specs=(P(None, "fluid", "sect", None), P("fluid", "sect"), P(("fluid", "sect"), None)),
        check_vma=False,
    )
```

```python
import jax
import jax.numpy as jnp
from jax import lax
from jax.experimental import pallas as pl
from jax.experimental.pallas import tpu as pltpu
from jax.sharding import PartitionSpec as P

STEP_FLUID = 0.045
STEP_DECK = 0.06
GAMMA_LESS = 0.4
AMBIENT = 1.0

TABLE = 64
DECK = 72
EDGES = 80
BLOCK = 120
PER = 7
VALUES = 64
NT = (((1,), (1,)), ((), ()))
NN = (((1,), (0,)), ((), ()))


def local_call(kernel, shapes, name, args, scratch=(), flops=1_000_000, smem=(), hbm=(), out_hbm=(), free=False):
    outs = [jax.ShapeDtypeStruct(*s) if free else pltpu.HBM(*s) if i in out_hbm else pltpu.VMEM(*s) for i, s in enumerate(shapes)]
    spaces = [pltpu.SMEM if i in smem else pltpu.HBM if i in hbm else pltpu.VMEM for i in range(len(args))]
    args = [pltpu.with_memory_space_constraint(a, pltpu.HBM) if i in hbm else a for i, a in enumerate(args)]
    return pl.pallas_call(
        kernel,
        out_shape=outs,
        in_specs=[pl.BlockSpec(memory_space=s) for s in spaces],
        out_specs=[pl.BlockSpec(memory_space=pltpu.HBM if i in out_hbm else pltpu.VMEM) for i in range(len(outs))],
        scratch_shapes=list(scratch),
        compiler_params=pltpu.CompilerParams(vmem_limit_bytes=32 * 1024 * 1024),
        cost_estimate=pl.CostEstimate(flops=flops, bytes_accessed=1_000_000, transcendentals=0),
        name=name,
    )(*args)


def floats(*shape):
    return shape, jnp.float32


def iota(shape, axis):
    return lax.broadcasted_iota(jnp.int32, shape, axis)


def split3(x):
    high = x.astype(jnp.bfloat16)
    rest = x - high.astype(jnp.float32)
    middle = rest.astype(jnp.bfloat16)
    low = (rest - middle.astype(jnp.float32)).astype(jnp.bfloat16)
    return high, middle, low


def pick(onehot, table, dims=NN):
    onehot = onehot.astype(jnp.float32).astype(jnp.bfloat16)
    total = None
    for part in split3(table):
        term = lax.dot_general(onehot, part, dims, preferred_element_type=jnp.float32)
        total = term if total is None else total + term
    return total


YOFF = 8
YROWS = 80
KFL = 0.5 * STEP_FLUID


def euler_prims(rho, m1, m2, m3, en):
    inv = 1.0 / rho
    v1, v2, v3 = m1 * inv, m2 * inv, m3 * inv
    p = GAMMA_LESS * (en - 0.5 * (m1 * v1 + m2 * v2 + m3 * v3))
    return v1, v2, v3, p, jnp.sqrt(1.4 * p * inv)


def from_raw(rho, v1, v2, v3, p):
    en = p * (1.0 / GAMMA_LESS) + 0.5 * rho * (v1 * v1 + v2 * v2 + v3 * v3)
    return (rho, rho * v1, rho * v2, rho * v3, en), (v1, v2, v3, p, jnp.sqrt(1.4 * p / rho))


def flux(state, prim, d):
    rho, m1, m2, m3, en = state
    v, p = prim[d], prim[3]
    out = [state[1 + d], m1 * v, m2 * v, m3 * v, (en + p) * v]
    out[1 + d] = out[1 + d] + p
    return out


def add_direction(acc, here, prim, up, uprim, down, dprim, d):
    fu, fd = flux(up, uprim, d), flux(down, dprim, d)
    s0 = jnp.abs(prim[d]) + prim[4]
    lu = jnp.maximum(s0, jnp.abs(uprim[d]) + uprim[4])
    ld = jnp.maximum(s0, jnp.abs(dprim[d]) + dprim[4])
    out = []
    for c in range(5):
        term = (fu[c] - fd[c]) - lu * (up[c] - here[c]) + ld * (here[c] - down[c])
        out.append(term if acc is None else acc[c] + term)
    return out


def prep_kernel(rho_hbm, vel_hbm, pre_hbm, w_hbm, u_hbm, cells_hbm, owner_hbm, row_hbm, raw_ref, wu_ref, ext_ref, cor_ref, own_ref, cells_ref, slots_ref, sems):
    core = lax.axis_index("fluid") % 2
    pairs = [
        (rho_hbm, raw_ref.at[0]),
        (vel_hbm, raw_ref.at[pl.ds(1, 3)]),
        (pre_hbm, raw_ref.at[4]),
        (w_hbm, wu_ref.at[0]),
        (u_hbm, wu_ref.at[1]),
        (cells_hbm, cells_ref),
        (owner_hbm, slots_ref.at[pl.ds(0, 1)]),
        (row_hbm, slots_ref.at[pl.ds(8, 1)]),
    ]
    copies = [pltpu.make_async_copy(a, b, sems.at[i]) for i, (a, b) in enumerate(pairs)]
    for copy in copies:
        copy.start()
    chooser = iota((16, 128), 0) == iota((16, 128), 1)
    own_ref[15:16, :] = jnp.zeros((1, 256), jnp.float32)
    ext_ref[22:24, :] = jnp.zeros((2, 128), jnp.float32)
    cor_ref[22:24, :] = jnp.zeros((2, 128), jnp.float32)
    for copy in copies[:5]:
        copy.wait()
    thin = pick(chooser, raw_ref[...].reshape(1280, 128), NT)
    for c in range(5):
        own_ref[3 * c : 3 * c + 3, :] = thin[0:3, 256 * c : 256 * c + 256]
    first, last = own_ref[:, 0:128], own_ref[:, 128:256]
    even = core == 0
    ext_ref[0:16, :] = jnp.where(even, first, last)
    cor_ref[0:16, :] = jnp.where(even, last, first)
    wf, wl, uf, ul = wu_ref[0, 0:4, :], wu_ref[0, 60:64, :], wu_ref[1, 0:2, :], wu_ref[1, 62:64, :]
    ext_ref[16:20, :] = jnp.where(even, wf, wl)
    cor_ref[16:20, :] = jnp.where(even, wl, wf)
    ext_ref[20:22, :] = jnp.where(even, uf, ul)
    cor_ref[20:22, :] = jnp.where(even, ul, uf)
    for copy in copies[5:]:
        copy.wait()


def table_kernel(cells_ref, slots_ref, raw_ref, count_ref, tab_ref, choose_ref, place_ref, edge_ref):
    for c in range(5):
        for side, y in ((0, 0), (1, 62)):
            for i in range(4):
                edge_ref[side, pl.ds(8 * c + 2 * i, 2), :] = raw_ref[c, i, pl.ds(y, 2), :]
    owner_row = jnp.broadcast_to(slots_ref[0:1, :].astype(jnp.float32), (128, 128))
    owner = owner_row.T
    same = owner == owner_row
    down, along = iota((128, 128), 0), iota((128, 128), 1)
    within = jnp.sum(jnp.where(same & (along < down), 1.0, 0.0), axis=1, keepdims=True)
    within_row = jnp.sum(jnp.where(same & (down < along), 1.0, 0.0), axis=0, keepdims=True)
    position = (2.0 * owner[:, 0:1] + within).astype(jnp.int32)
    whole, spot = by_seven(iota((64 * PER, 128), 0))
    position_row = (2.0 * owner_row[0:1, :] + within_row).astype(jnp.int32)
    choose = (position_row == 2 * whole + spot - 2) & (spot < 6)
    choose_ref[...] = choose.astype(jnp.float32).astype(jnp.bfloat16)
    place = jnp.where(position == along, 1.0, 0.0).astype(jnp.bfloat16)
    place_ref[...] = place
    r, c = iota((16, 128), 0), iota((16, 128), 1)
    columns = jnp.where(((r < 2) & (c == r)) | ((r >= 2) & (r < 4) & (c == r + 124)), 1.0, 0.0).astype(jnp.bfloat16)
    cells = cells_ref[...].astype(jnp.float32).astype(jnp.bfloat16)
    picked = lax.dot_general(columns, cells, NT, preferred_element_type=jnp.float32)
    live = iota((1, 128), 1) < count_ref[...]
    code = jnp.where(live, slots_ref[8:9, :] + 128, 0).astype(jnp.float32)
    stacked = jnp.where(r == 4, jnp.broadcast_to(code, (16, 128)), picked).astype(jnp.bfloat16)
    tab_ref[...] = lax.dot_general(stacked, place, NN, preferred_element_type=jnp.float32)[0:8]


def middle_kernel(ext_ref, cor_ref, own_ref, wu_ref, tab_ref, edge_ref, up_ref, down_ref, far_ref, deck_ref, wide):
    fluid = lax.axis_index("fluid")
    even = fluid % 2 == 0
    ext, cor = ext_ref[...], cor_ref[...]
    low, high = jnp.where(even, ext, cor), jnp.where(even, cor, ext)
    low_deck = jnp.where(fluid == 0, 0.0, low[16:24])
    high_deck = jnp.where(fluid == 63, 0.0, high[16:24])
    wide[...] = jnp.zeros((2, 128, 128), jnp.float32)
    wide[0, 4:8, :] = low_deck[0:4]
    wide[0, 8:72, :] = wu_ref[0]
    wide[0, 72:76, :] = high_deck[0:4]
    wide[1, 6:8, :] = low_deck[4:6]
    wide[1, 8:72, :] = wu_ref[1]
    wide[1, 72:74, :] = high_deck[4:6]
    deck_ref[...] = wide[:, 0:80, :]
    w_columns, u_columns = wide[0].T, wide[1].T
    tiles = [low[0:16], own_ref[:, 0:128], own_ref[:, 128:256], high[0:16]]
    pad = jnp.zeros((2, 128), jnp.float32)
    for ref, side, w_part, u_part in ((up_ref, 1, w_columns[124:128], u_columns[126:128]), (down_ref, 0, w_columns[0:4], u_columns[0:2])):
        ref[0:80, :] = jnp.concatenate(tiles + [tab_ref[...], w_part, u_part, pad], axis=0)
        ref[EDGES:BLOCK, :] = edge_ref[side]
    y = iota((16, 128), 1) & 63
    rim = (y < 2) | (y >= 62)
    far_ref[...] = sum(pltpu.roll(jnp.where(rim, x, 0.0), 4 * i, 1) if i else jnp.where(rim, x, 0.0) for i, x in enumerate(tiles))


def wall_press(thin):
    lane = iota((8, 128), 1)
    low_half, y = lane < 64, lane & 63

    def get(t, c, z):
        part = thin[pl.ds(16 * t + 3 * c + z, 4, stride=64), :]
        return jnp.concatenate([part, part], axis=0)

    def x_around(tiles):
        turned = [pltpu.roll(x, 64, 1) for x in tiles]
        after, before = turned[1:] + turned[-1:], turned[:1] + turned[:-1]
        ups = [jnp.where(low_half, a, b) for a, b in zip(turned, after)]
        downs = [jnp.where(low_half, b, a) for a, b in zip(turned, before)]
        return ups, downs

    def y_up(x):
        return jnp.where(y == 63, pltpu.roll(pltpu.roll(x, 7, 0), 63, 1), pltpu.roll(x, 127, 1))

    def y_down(x):
        return jnp.where(y == 0, pltpu.roll(pltpu.roll(x, 1, 0), 65, 1), pltpu.roll(x, 1, 1))

    def mirrored(state, prim):
        return [state[0], state[1], state[2], -state[3], state[4]], [prim[0], prim[1], -prim[2], prim[3], prim[4]]

    def advance(states, prims, layer, tiles):
        here, q = states[layer], prims[layer]
        xu = [x_around([here[t][c] for t in range(4)]) for c in range(5)]
        xq = {c: x_around([q[t][c] for t in range(4)]) for c in (0, 3, 4)}
        result = []
        for t in tiles:
            pack = [None] * 5
            up, down = [xu[c][0][t] for c in range(5)], [xu[c][1][t] for c in range(5)]
            upq, downq = list(pack), list(pack)
            for c in (0, 3, 4):
                upq[c], downq[c] = xq[c][0][t], xq[c][1][t]
            acc = add_direction(None, here[t], q[t], up, upq, down, downq, 0)
            up, down = [y_up(here[t][c]) for c in range(5)], [y_down(here[t][c]) for c in range(5)]
            upq, downq = list(pack), list(pack)
            for c in (1, 3, 4):
                upq[c], downq[c] = y_up(q[t][c]), y_down(q[t][c])
            acc = add_direction(acc, here[t], q[t], up, upq, down, downq, 1)
            down, downq = mirrored(here[t], q[t]) if layer == 0 else (states[layer - 1][t], prims[layer - 1][t])
            acc = add_direction(acc, here[t], q[t], states[layer + 1][t], prims[layer + 1][t], down, downq, 2)
            result.append([here[t][c] - KFL * acc[c] for c in range(5)])
        return result

    states, prims = [], []
    for z in range(3):
        both = [from_raw(*[get(t, c, z) for c in range(5)]) for t in range(4)]
        states.append([b[0] for b in both])
        prims.append([b[1] for b in both])
    after = [advance(states, prims, z, range(4)) for z in range(2)]
    after_prims = [[euler_prims(*after[z][t]) for t in range(4)] for z in range(2)]
    final = advance(after, after_prims, 0, (1, 2))
    return [euler_prims(*final[i])[3] for i in range(2)]


def by_seven(k):
    whole = (k * 9363) >> 16
    return whole, k - PER * whole


def gather_lanes(tables, cells):
    index = cells & 127
    low = jnp.take_along_axis(jnp.broadcast_to(tables[0], cells.shape), index, axis=1, mode="promise_in_bounds")
    high = jnp.take_along_axis(jnp.broadcast_to(tables[1], cells.shape), index, axis=1, mode="promise_in_bounds")
    return jnp.where(cells < 128, low, high) - AMBIENT


def facet_kernel(up_ref, left_ref, right_ref, far_ref, cells_ref, tab_ref, choose_ref, out_hbm, thin, press, out_ref, sems):
    sect = lax.axis_index("sect")
    for i, ref in ((0, up_ref), (1, right_ref), (3, left_ref)):
        thin[64 * i : 64 * i + 64, :] = ref[0:64, :]
    far = far_ref[...]
    for i in range(4):
        thin[128 + 16 * i : 144 + 16 * i, :] = pltpu.roll(far, 128 - 4 * i, 1) if i else far
    first, second = wall_press(thin)
    press[0:8, :] = first
    press[8:16, :] = second

    def tables(s):
        return press[s : s + 1, :], press[s + 8 : s + 9, :]

    left_tab, right_tab = left_ref[TABLE : TABLE + 8, :], right_ref[TABLE : TABLE + 8, :]
    left_values = gather_lanes(tables(3), left_tab.astype(jnp.int32))
    right_values = gather_lanes(tables(1), right_tab.astype(jnp.int32))
    left_code = jnp.where(sect == 0, 0.0, left_tab[4:5])
    right_code = jnp.where(sect == 3, 0.0, right_tab[4:5])
    codes = jnp.concatenate([jnp.broadcast_to(x, (8, 128)) for x in (tab_ref[4:5, :], left_code, right_code)], axis=0)
    four = jnp.concatenate([left_values[2:4], right_values[0:2]], axis=0)
    eight = jnp.concatenate([four, four], axis=0)

    def weights(i):
        here = jnp.where((iota((24, 128), 0) & 7) == 2 + i, codes, 0.0)
        there = jnp.where((iota((8, 128), 0) >> 2) == i, eight, 0.0)
        return jnp.concatenate([here, jnp.zeros((48, 128), jnp.float32), there, jnp.zeros((48, 128), jnp.float32)], axis=0)

    o, p = iota((64, 256), 0), iota((64, 256), 1)
    base = pick(2 * o + (p >> 7) == (p & 127), jnp.concatenate([weights(0), weights(1)], axis=1), NT)
    owner, in_codes = iota((64, 128), 0), iota((64, 128), 1) < VALUES
    before = jnp.where(owner == 0, 0.0, pltpu.roll(base, 1, 0))
    after = jnp.where(owner == 63, 0.0, pltpu.roll(base, 63, 0))
    meta = base + jnp.where(in_codes, pltpu.roll(before, 126, 1), pltpu.roll(before, 120, 1))
    meta = meta + jnp.where(in_codes, pltpu.roll(after, 2, 1), pltpu.roll(after, 8, 1))
    parts = split3(gather_lanes(tables(0), cells_ref[...]))
    copies = []
    size = 16 * PER
    for i in range(4):
        chooser = choose_ref[pl.ds(size * i, size), :]
        total = None
        for part in parts:
            term = lax.dot_general(chooser, part, NN, preferred_element_type=jnp.float32)
            total = term if total is None else total + term
        out_ref[pl.ds(size * i, size), :] = total
        out_ref[pl.ds(size * i + 6, 16, stride=PER), :] = meta[16 * i : 16 * i + 16]
        copies.append(pltpu.make_async_copy(out_ref.at[pl.ds(size * i, size)], out_hbm.at[pl.ds(size * i, size)], sems.at[i]))
        copies[-1].start()
    for copy in copies:
        copy.wait()


def spread_sides(x):
    lanes = x.shape[1]
    return pltpu.roll(x, 1, 1) + pltpu.roll(x, lanes - 1, 1)


def early_kernel(left_ref, right_ref, deck_ref, stiff_ref, tension_ref, anchor_ref, failed_ref, out_ref, turn):
    fluid, sect = lax.axis_index("fluid"), lax.axis_index("sect")
    turn[...] = jnp.zeros((2, 128, 128), jnp.float32)
    from_left = jnp.where(sect == 0, 0.0, left_ref[DECK : DECK + 8, :])
    from_right = jnp.where(sect == 3, 0.0, right_ref[DECK : DECK + 8, :])
    turn[0, 0:4, :] = from_right[0:4]
    turn[0, 124:128, :] = from_left[0:4]
    turn[1, 0:2, :] = from_right[4:6]
    turn[1, 126:128, :] = from_left[4:6]
    w = jnp.concatenate([deck_ref[0], turn[0].T[0:80]], axis=1)
    u = jnp.concatenate([deck_ref[1], turn[1].T[0:80]], axis=1)
    anchor = anchor_ref[...]
    count = anchor.shape[1]
    alive = iota((1, count), 1) != failed_ref[0]
    row = (anchor >> 9) - 64 * fluid + 8
    column = (anchor & 511) - 128 * sect
    lane = jnp.where((column >= -4) & (column < 132) & alive, column & 255, -1)
    rows = iota((80, count), 0) == row
    columns = iota((256, count), 0) == lane
    alpha = pick(rows, jnp.where(columns, stiff_ref[...], 0.0), NT)
    beta = pick(rows, jnp.where(columns, tension_ref[...], 0.0), NT)

    def laplace(x):
        return pltpu.roll(x, 1, 0) + pltpu.roll(x, 79, 0) + spread_sides(x) - 4.0 * x

    first = 2.0 * w - u + STEP_DECK * (beta - alpha * w - laplace(laplace(w)))
    r, c = iota((80, 256), 0) - 8, iota((80, 256), 1)
    c = jnp.where(c < 132, c, c - 256)
    g, h = r + 64 * fluid, c + 128 * sect
    inside = (g >= 0) & (g < 4096) & (h >= 0) & (h < 512) & (c >= -2) & (c < 130) & (r >= -2) & (r < 66)
    out_ref[0] = w
    out_ref[1] = jnp.where(inside, first, 0.0)
    out_ref[2] = alpha
    out_ref[3] = beta


def deck_kernel(got_ref, early_ref, deck_ref, ret_ref, spread, sides_ref, turn):
    count = 64 * PER
    meta = got_ref[pl.ds(6, 64, stride=PER), :]
    lane = iota((64, 128), 1)
    outer = (lane < 2) | (lane >= 126)
    for j in range(PER):
        spread[pl.ds(j, 64, stride=PER), :] = meta if j < 6 else jnp.zeros((64, 128), jnp.float32)
        turned = pltpu.roll(meta, (126 - VALUES - 4 * j) % 128, 1) if j < 6 else meta
        sides_ref[pl.ds(j, 64, stride=PER), :] = jnp.where(outer, turned, 0.0) if j < 6 else jnp.zeros((64, 128), jnp.float32)
    c = iota((count, 128), 1)
    own = jnp.where(((c & 7) == by_seven(iota((count, 128), 0))[1]) & (c < 24), spread[...], 0.0).astype(jnp.bfloat16)
    chooser = ((iota((16, 128), 1) >> 3) == iota((16, 128), 0)).astype(jnp.float32).astype(jnp.bfloat16)
    codes = lax.dot_general(chooser, own, NT, preferred_element_type=jnp.float32).astype(jnp.int32)
    place = by_seven(iota((1, count), 1))[1]
    offset = 64 * (place >> 1) - 64 + 8 - 128

    def rows_of(which):
        code = codes[which : which + 1]
        local = jnp.where(code > 0, code + offset, -1)
        return iota((80, count), 0) == local

    centre = pick(rows_of(0), got_ref[...])
    sides = pick(jnp.concatenate([rows_of(1), rows_of(2)], axis=0), sides_ref[...])
    edge = iota((80, 128), 1)
    sides = jnp.where(edge >= 126, sides[0:80], jnp.where(edge < 2, sides[80:160], 0.0))
    load = jnp.concatenate([centre, sides], axis=1)
    first = early_ref[1] + STEP_DECK * load
    turn[8:88, :] = first

    def at(step):
        return turn[16 + step : 80 + step, :]

    here = at(0)
    near, two = at(1) + at(-1), at(2) + at(-2)
    cross = 2.0 * near - 8.0 * here
    bend = 20.0 * here - 8.0 * near + two
    for x, step in ((cross, 1), (here, 2)):
        bend = bend + pltpu.roll(x, step, 1) + pltpu.roll(x, 256 - step, 1)
    bend = bend[:, 0:128]
    own_rows = slice(8, 72)
    here = here[:, 0:128]
    force = centre[own_rows] + early_ref[3, own_rows, 0:128] - early_ref[2, own_rows, 0:128] * here
    tile = 2.0 * here - early_ref[0, own_rows, 0:128] + STEP_DECK * (force - bend)
    deck_ref[...] = tile
    row = jnp.concatenate([meta[:, 2:3], meta[:, 3:4]], axis=0).astype(jnp.int32) - 128
    answer = pick(iota((128, 64), 1) == row, tile)
    for i in range(2):
        ret_ref[:, i, :] = answer[64 * i : 64 * i + 64]


def final_kernel(got_ref, place_ref, out_ref):
    out_ref[...] = pick(place_ref[...], got_ref[...])


def pack_kernel(raw_ref, left_ref, right_ref, ext_ref, cor_ref):
    core = lax.axis_index("fluid") % 2
    for ref, start in ((ext_ref, 2 * core), (cor_ref, 2 - 2 * core)):
        for c in range(5):
            for i in range(2):
                ref[c, i, 0:64, :] = raw_ref[c, start + i]
                ref[c, i, 64:66, :] = right_ref[pl.ds(EDGES + 8 * c + 2 * (start + i), 2), :]
                ref[c, i, 66:68, :] = left_ref[pl.ds(EDGES + 8 * c + 2 * (start + i), 2), :]
                ref[c, i, 68:72, :] = jnp.ones((4, 128), jnp.float32)


def bulk_kernel(raw_ref, ext_ref, cor_ref, left_ref, right_ref, tile_ref, out_hbm, deck_hbm, ua, pa, ub, pb, result, sems):
    deck_copy = pltpu.make_async_copy(tile_ref, deck_hbm, sems.at[4])
    deck_copy.start()
    core = lax.axis_index("fluid") % 2
    lane = lax.broadcasted_iota(jnp.int32, (8, 128), 1)
    first, last = lane == 0, lane == 127

    def put(planes, rows, raw):
        state, prim = from_raw(*raw)
        for c in range(5):
            ua[c, planes, rows, :] = state[c]
            pa[c, planes, rows, :] = prim[c]

    def own(i, _):
        for r in range(0, 64, 8):
            rows = pl.ds(r, 8)
            put(i + 2, pl.ds(r + YOFF, 8), [raw_ref[c, i, rows, :] for c in range(5)])
        put(i + 2, pl.ds(YOFF - 2, 2), [left_ref[pl.ds(EDGES + 8 * c + 2 * i, 2), :] for c in range(5)])
        put(i + 2, pl.ds(YOFF + 64, 2), [right_ref[pl.ds(EDGES + 8 * c + 2 * i, 2), :] for c in range(5)])
        return 0

    lax.fori_loop(0, 4, own, 0)

    def halo(i, _):
        for ref, base in ((ext_ref, 6 * core), (cor_ref, 6 - 6 * core)):
            for r in range(0, 64, 8):
                put(base + i, pl.ds(r + YOFF, 8), [ref[c, i, pl.ds(r, 8), :] for c in range(5)])
            put(base + i, pl.ds(YOFF + 64, 2), [ref[c, i, pl.ds(64, 2), :] for c in range(5)])
            put(base + i, pl.ds(YOFF - 2, 2), [ref[c, i, pl.ds(66, 2), :] for c in range(5)])
        return 0

    lax.fori_loop(0, 2, halo, 0)

    def update(u, q, i, r, n):
        def load(plane, row):
            rows = pl.ds(row, n)
            return [u[c, plane, rows, :] for c in range(5)], [q[c, plane, rows, :] for c in range(5)]

        here, prim = load(i, r)
        acc = None
        for d, (up, down) in enumerate((((i + 1, r), (i - 1, r)), ((i, r + 1), (i, r - 1)))):
            uu, uq = load(*up)
            du, dq = load(*down)
            acc = add_direction(acc, here, prim, uu, uq, du, dq, d)

        def shifted(x, sign, step, edge):
            return jnp.where(edge[:n], sign * x if sign < 0 else x, pltpu.roll(x, step, 1))

        signs = (1, 1, 1, -1, 1)
        qsigns = (None, None, -1, 1, 1)
        zu = [shifted(here[c], signs[c], 127, last) for c in range(5)]
        zd = [shifted(here[c], signs[c], 1, first) for c in range(5)]
        zuq = [None if qsigns[c] is None else shifted(prim[c], qsigns[c], 127, last) for c in range(5)]
        zdq = [None if qsigns[c] is None else shifted(prim[c], qsigns[c], 1, first) for c in range(5)]
        acc = add_direction(acc, here, prim, zu, zuq, zd, zdq, 2)
        return [here[c] - KFL * acc[c] for c in range(5)]

    def step_one(i, _):
        for r, n in [(YOFF - 8, 8)] + [(YOFF + k, 8) for k in range(0, 72, 8)]:
            if r == YOFF - 8:
                r, n = YOFF - 1, 1
            if r == YOFF + 64:
                n = 1
            new = update(ua, pa, i, r, n)
            prim = euler_prims(*new)
            for c in range(5):
                ub[c, i, pl.ds(r, n), :] = new[c]
                pb[c, i, pl.ds(r, n), :] = prim[c]
        return 0

    lax.fori_loop(1, 7, step_one, 0)

    def step_two(i, _):
        for r in range(0, 64, 8):
            new = update(ub, pb, i + 2, r + YOFF, 8)
            for c in range(5):
                result[c, i, pl.ds(r, 8), :] = new[c]
        return 0

    copies = []
    for i in range(4):
        step_two(i, 0)
        copies.append(pltpu.make_async_copy(result.at[:, i], out_hbm.at[:, i], sems.at[i]))
        copies[-1].start()
    for copy in copies:
        copy.wait()
    deck_copy.wait()


def bulk_euler(raw, ext, cor, left, right, tile):
    return local_call(
        bulk_kernel,
        [floats(5, 4, 64, 128), floats(64, 128)],
        "bulk_euler",
        (raw, ext, cor, left, right, tile),
        scratch=[pltpu.VMEM((5, 8, YROWS, 128), jnp.float32)] * 4 + [pltpu.VMEM((5, 4, 64, 128), jnp.float32), pltpu.SemaphoreType.DMA((5,))],
        flops=60_000_000,
        out_hbm=(0, 1),
    )


def body(
    density,
    velocity,
    pressure,
    deck_disp,
    deck_prev,
    stay_stiff,
    stay_tension,
    anchor_node,
    failed_stay,
    facet_cells,
    facet_owner,
    facet_row,
    facet_count,
):
    count = lax.axis_size("fluid")
    outward = [(i, (i + 1) % count if i % 2 else (i - 1) % count) for i in range(count)]
    inward = [(i, i ^ 1) for i in range(count)]
    raw, wu, ext, cor, own, cells, slots = local_call(
        prep_kernel,
        [floats(5, 4, 64, 128), floats(2, 64, 128), floats(24, 128), floats(24, 128), floats(16, 256), ((128, 128), jnp.int32), ((16, 128), jnp.int32)],
        "prep",
        (density, velocity, pressure, deck_disp, deck_prev, facet_cells, facet_owner.reshape(1, -1), facet_row.reshape(1, -1)),
        scratch=[pltpu.SemaphoreType.DMA((8,))],
        hbm=range(8),
    )
    ext = lax.ppermute(ext, "fluid", outward)
    cor = lax.ppermute(cor, "fluid", inward)
    tab, choose, place, edge = local_call(
        table_kernel, [floats(8, 128), ((64 * PER, 128), jnp.bfloat16), ((128, 128), jnp.bfloat16), floats(2, 40, 128)], "tables", (cells, slots, raw, facet_count.reshape(1, 1))
    )
    up, down, far, deck = local_call(
        middle_kernel,
        [floats(BLOCK, 128), floats(BLOCK, 128), floats(16, 128), floats(2, 80, 128)],
        "middle",
        (ext, cor, own, wu, tab, edge),
        scratch=[pltpu.VMEM((2, 128, 128), jnp.float32)],
    )
    around = lax.axis_size("sect")
    forward = [(i, (i + 1) % around) for i in range(around)]
    backward = [(i, (i - 1) % around) for i in range(around)]
    far = lax.ppermute(far, "sect", [(i, (i + 2) % around) for i in range(around)])
    left = lax.ppermute(up, "sect", forward)
    right = lax.ppermute(down, "sect", backward)
    (facets,) = local_call(
        facet_kernel,
        [floats(64 * PER, 128)],
        "facets",
        (up, left, right, far, cells, tab, choose),
        scratch=[pltpu.VMEM((256, 128), jnp.float32), pltpu.VMEM((16, 128), jnp.float32), pltpu.VMEM((64 * PER, 128), jnp.float32), pltpu.SemaphoreType.DMA((4,))],
        flops=4_000_000,
        out_hbm=(0,),
    )
    got = lax.all_to_all(facets.reshape(64, 1, PER * 128), "fluid", split_axis=0, concat_axis=0, tiled=True).reshape(64 * PER, 128)
    (early,) = local_call(
        early_kernel,
        [floats(4, 80, 256)],
        "early_deck",
        (left, right, deck, stay_stiff.reshape(1, -1), stay_tension.reshape(1, -1), anchor_node.reshape(1, -1), failed_stay),
        scratch=[pltpu.VMEM((2, 128, 128), jnp.float32)],
        smem=(6,),
    )
    ext_planes, cor_planes = local_call(pack_kernel, [floats(5, 2, 72, 128), floats(5, 2, 72, 128)], "pack", (raw, left, right))
    ext_planes = lax.ppermute(ext_planes, "fluid", outward)
    cor_planes = lax.ppermute(cor_planes, "fluid", inward)
    tile, back = local_call(
        deck_kernel,
        [floats(64, 128), floats(64, 2, 128)],
        "deck",
        (got, early),
        scratch=[pltpu.VMEM((64 * PER, 128), jnp.float32)] * 2 + [pltpu.VMEM((96, 256), jnp.float32)],
        flops=4_000_000,
    )
    back = lax.all_to_all(back, "fluid", split_axis=0, concat_axis=0, tiled=True)
    fields, deck_next = bulk_euler(raw, ext_planes, cor_planes, left, right, tile)
    (facet_disp,) = local_call(final_kernel, [floats(128, 128)], "final", (back.reshape(128, 128), place), free=True)
    return (fields, deck_next, facet_disp)


def solution(mesh):
    return jax.shard_map(
        body,
        mesh=mesh,
        in_specs=(
            P("fluid", "sect", None),
            P(None, "fluid", "sect", None),
            P("fluid", "sect", None),
            P("fluid", "sect"),
            P("fluid", "sect"),
            P(),
            P(),
            P(),
            P(),
            P(("fluid", "sect"), None),
            P(("fluid", "sect"), None),
            P(("fluid", "sect")),
            P(("fluid", "sect")),
        ),
        out_specs=(P(None, "fluid", "sect", None), P("fluid", "sect"), P(("fluid", "sect"), None)),
        check_vma=False,
    )
```
